32 devices in a mesh: grp: 2 (over y), gx: 4 (over z), gy: 2 (over x), gz: 2 (over core).
Axes of the slice: x: 2, y: 2, z: 4, core: 2. Of those that a mesh axis runs over, the one named last changes fastest.
Arguments:
- hidden_in: bfloat16 [64, 18432], P(('grp', 'gy', 'gz'), 'gx'), parts along dimension 0
- ln_gain: float32 [18432], P('gx'), may hold values from 0.1 to 1.9
- w_query: bfloat16 [18432, 12288], P('gx', ('gy', 'gz')), may hold values from -0.046875 to 0.046875
- w_keyval: bfloat16 [18432, 512], P('gx', ('gy', 'gz')), may hold values from -0.046875 to 0.046875
- w_output: bfloat16 [12288, 18432], P(('gy', 'gz'), 'gx'), may hold values from -0.3125 to 0.3125
- key_cache: bfloat16 [64, 512, 256], P(('grp', 'gx', 'gy', 'gz')), parts along dimension 0, as said below
- value_cache: bfloat16 [64, 512, 256], P(('grp', 'gx', 'gy', 'gz')), parts along dimension 0, may hold values from -6 to 6
- lengths: int32 [64], P(('grp', 'gx', 'gy', 'gz')), parts along dimension 0, may hold values from 1 to 512, as said below
- positions: int32 [64], P(('grp', 'gx', 'gy', 'gz')), parts along dimension 0, may hold values from 0 to 8191
Outputs:
- attn_out: float32 [64, 18432], P(('grp', 'gy', 'gz'), 'gx'), parts along dimension 0
The draws below stay inside these ranges and needn't reach their ends.
There are 2 independent parts, one for each index of `grp`. The reference program is written for one: setup_inputs(seed, part) draws one part's arguments, and reference() takes and returns one part's arrays. A program takes and returns all parts, laid end to end along the dimension named above; an argument that names none is the same for every part. Nothing has to cross between parts.
Inputs may be any that keep to these rules, and one draw needn't show every extreme that they name: Each sequence attends to its first lengths cache slots and its new token; in every draw some sequence uses all 512 slots. `key_cache`: keys already carry their rotary positions.
All inputs are finite; a program needn't handle non-finite values.
Results may differ from the reference program's by a relative error of at most 0.012.
The reference program's roundings to bfloat16 on the way (of `normed`, `projected`, `query`, `rot_query`, `probs` and `heads`) count: a program that leaves them out, or rounds other values in their place, can miss the bound.
Values may be sent and summed in bfloat16 or wider, within the bound.
A program may use at most 128 MiB of HBM per device.

```python
import math
import jax
import jax.numpy as jnp
from jax import lax

D = 18432
HQ = 48
DH = 256
CACHE_LEN = 512
BATCH = 32
HEAD_BLK = 3072


def draw_hidden_in(key, part):
    key = jax.random.fold_in(key, 11)
    first, second, third = jax.random.split(key, 3)
    rising = 3.0 ** (jnp.arange(D, dtype=jnp.float32) / (D - 1))
    columns = rising * jnp.exp(jax.random.uniform(second, (D,), jnp.float32, 0.0, math.log(4.0)))
    rowscale = jnp.exp(jax.random.uniform(third, (BATCH, 1), jnp.float32, 0.0, math.log(10.0)))
    base = jax.random.normal(first, (BATCH, D), jnp.float32)
    return (0.25 * base * columns[None, :] * rowscale).astype(jnp.bfloat16)


def draw_key_cache(key, part):
    key = jax.random.fold_in(key, 12)
    first = jax.random.fold_in(key, 0)
    base = jax.random.normal(first, (BATCH, CACHE_LEN, DH), jnp.float32)
    base = jnp.clip(base, -6.0, 6.0)
    return base.astype(jnp.bfloat16)


def draw_lengths(key, part):
    key = jax.random.fold_in(key, 13)
    first, second = jax.random.split(key)
    drawn = jax.random.randint(first, (BATCH,), 1, CACHE_LEN + 1)
    chosen = jax.random.randint(second, (), 0, BATCH)
    return jnp.where(jnp.arange(BATCH, dtype=jnp.int32) == chosen, CACHE_LEN, drawn).astype(jnp.int32)


def with_ends(entries, key, least, top_value):
    longest = entries.shape.index(max(entries.shape))
    spots = []
    for shift in (0, 1):
        where = [jax.random.randint(jax.random.fold_in(key, axis), (), 0, length) for axis, length in enumerate(entries.shape)]
        where[longest] = (where[longest] + shift) % entries.shape[longest]
        spots.append(tuple(where))
    return entries.at[spots[0]].set(least).at[spots[1]].set(top_value)


def steps_of(rng, dims, pieces, low, largest):
    level = 1.0
    for dim, blocks in pieces:
        steps = jax.random.uniform(jax.random.fold_in(jax.random.fold_in(rng, 6), dim), (blocks,), jnp.float32, low / len(pieces), largest / len(pieces))
        level = level * jnp.repeat(jnp.exp(steps), dims[dim] // blocks).reshape((-1,) + (1,) * (len(dims) - 1 - dim))
    return level


def noise(rng, dims, deviation, limit, cuts=(), kind=jnp.bfloat16):
    result = jax.random.normal(rng, dims, jnp.float32) * deviation
    if len(cuts) > 0:
        result = steps_of(rng, dims, cuts, -0.22, 0.18) * result
    return jnp.clip(result, min=-limit, max=limit).astype(kind)


def setup_inputs(seed: int = 0, part: int = 0) -> dict:
    streams_of = jax.random.split(jax.random.key(seed), 10)
    own_keys = jax.random.split(jax.random.fold_in(streams_of[9], part), 10)
    hidden_in = draw_hidden_in(jax.random.fold_in(jax.random.fold_in(streams_of[9], part), 71), part)
    ln_gain = jnp.clip(1.0 + 0.18 * jax.random.normal(streams_of[1], (D,), jnp.float32), 0.1, 1.9)
    w_query = noise(streams_of[2], (D, HQ * DH), D ** -0.5, 0.046875, ((0, 4), (1, 4)))
    w_keyval = noise(streams_of[3], (D, 2 * DH), D ** -0.5, 0.046875, ((0, 4), (1, 4)))
    w_output = noise(streams_of[4], (HQ * DH, D), (HQ * DH // 32) ** -0.5, 0.3125, ((0, 4), (1, 4)))
    key_cache = draw_key_cache(jax.random.fold_in(jax.random.fold_in(streams_of[9], part), 71), part)
    value_cache = noise(own_keys[6], (BATCH, CACHE_LEN, DH), 1.0, 6.0, ((0, 16),))
    lengths = draw_lengths(jax.random.fold_in(jax.random.fold_in(streams_of[9], part), 71), part)
    positions = with_ends(jax.random.randint(own_keys[8], (BATCH,), 0, 8192), jax.random.fold_in(own_keys[8], 1), 0, 8191).astype(jnp.int32)
    return {"hidden_in": hidden_in, "ln_gain": ln_gain, "w_query": w_query, "w_keyval": w_keyval, "w_output": w_output, "key_cache": key_cache, "value_cache": value_cache, "lengths": lengths, "positions": positions}


def rotary(values, places):
    half = values.shape[-1] // 2
    freqs = jnp.exp(-jnp.log(10000.0) * jnp.arange(half, dtype=jnp.float32) / half)
    angles = places.astype(jnp.float32)[:, None] * freqs[None, :]
    while angles.ndim < values.ndim:
        angles = angles[:, None, :]
    cosine = jnp.cos(angles)
    sine = jnp.sin(angles)
    first = values[..., :half]
    second = values[..., half:]
    return jnp.concatenate([first * cosine - second * sine, second * cosine + first * sine], -1)

def attend(query2d, keyval2d, key_cache, value_cache, lengths, positions):
    count = query2d.shape[0]
    heads_here = query2d.shape[1] // DH
    query = query2d.reshape(count, heads_here, DH).astype(jnp.float32)
    rot_query = rotary(query, positions).astype(jnp.bfloat16)
    rot_key = rotary(keyval2d[:, :DH].astype(jnp.float32), positions).astype(jnp.bfloat16)
    new_value = keyval2d[:, DH:]
    scale = DH ** (-0.5)
    scores = jnp.einsum('bhd,bld->bhl', rot_query.astype(jnp.float32), key_cache.astype(jnp.float32)) * scale
    selfish = jnp.einsum('bhd,bd->bh', rot_query.astype(jnp.float32), rot_key.astype(jnp.float32)) * scale
    live = jnp.arange(key_cache.shape[1], dtype=jnp.int32)[None, :] < lengths[:, None]
    live = live[:, None, :]
    masked = jnp.where(live, scores, -1e+30)
    peak = jnp.maximum(lax.optimization_barrier(jnp.max(masked, -1)), selfish)
    expo = jnp.where(live, jnp.exp(masked - peak[..., None]), 0.0)
    expo_self = jnp.exp(selfish - peak)
    total = lax.optimization_barrier(jnp.sum(expo, -1)) + expo_self
    probs = (expo / total[..., None]).astype(jnp.bfloat16)
    probs_self = (expo_self / total).astype(jnp.bfloat16)
    mixed = jnp.einsum('bhl,bld->bhd', probs.astype(jnp.float32), value_cache.astype(jnp.float32))
    mixed = mixed + probs_self.astype(jnp.float32)[..., None] * new_value.astype(jnp.float32)[:, None, :]
    return mixed.reshape(count, heads_here * DH).astype(jnp.bfloat16)

def reference(hidden_in, ln_gain, w_query, w_keyval, w_output, key_cache, value_cache, lengths, positions):
    xf = hidden_in.astype(jnp.float32)
    mean = lax.optimization_barrier(jnp.mean(xf, 1, keepdims=True))
    centered = xf - mean
    var = lax.optimization_barrier(jnp.mean(centered * centered, 1, keepdims=True))
    normed = (centered * lax.rsqrt(var + 1e-05) * ln_gain[None, :]).astype(jnp.bfloat16)
    first = jnp.dot(normed, w_query, preferred_element_type=jnp.float32)
    second = jnp.dot(normed, w_keyval, preferred_element_type=jnp.float32)
    projected = jnp.concatenate([first, second], 1).astype(jnp.bfloat16)
    heads = attend(projected[:, :HQ * DH], projected[:, HQ * DH:], key_cache, value_cache, lengths, positions)

    def add_block(total, index):
        start = (index * HEAD_BLK).astype(jnp.int32)
        cols_part = lax.dynamic_slice_in_dim(heads, start, HEAD_BLK, 1)
        weight_part = lax.dynamic_slice_in_dim(w_output, start, HEAD_BLK, 0)
        term = jnp.dot(cols_part, weight_part, preferred_element_type=jnp.float32)
        term = lax.optimization_barrier(term.astype(jnp.bfloat16)).astype(jnp.float32)
        return (total + term, None)
    blocks = HQ * DH // HEAD_BLK
    summed, _ = lax.scan(add_block, jnp.zeros((BATCH, D), jnp.float32), jnp.arange(blocks, dtype=jnp.int32))
    return summed
```

```python
import functools
import math

import jax
import jax.numpy as jnp
import numpy as np
from jax import lax
from jax.experimental import pallas as pl
from jax.experimental.pallas import tpu as pltpu
from jax.sharding import PartitionSpec as P

D = 18432
DH = 256
HALF = DH // 2
LANES = 128
MESH = pl.DeviceIdType.MESH
CHUNK_HEADS = 4
OUT_COLS = 768
SEQS = 2


def rotary(values, places):
    half = values.shape[-1] // 2
    freqs = jnp.exp(-jnp.log(10000.0) * jnp.arange(half, dtype=jnp.float32) / half)
    angles = places.astype(jnp.float32)[:, None] * freqs[None, :]
    while angles.ndim < values.ndim:
        angles = angles[:, None, :]
    cosine = jnp.cos(angles)
    sine = jnp.sin(angles)
    first = values[..., :half]
    second = values[..., half:]
    return jnp.concatenate([first * cosine - second * sine, second * cosine + first * sine], -1)


def attend(query2d, keyval2d, key_cache, value_cache, lengths, positions):
    count = query2d.shape[0]
    heads_here = query2d.shape[1] // DH
    query = query2d.reshape(count, heads_here, DH).astype(jnp.float32)
    rot_query = rotary(query, positions).astype(jnp.bfloat16)
    rot_key = rotary(keyval2d[:, :DH].astype(jnp.float32), positions).astype(jnp.bfloat16)
    new_value = keyval2d[:, DH:]
    scale = DH ** (-0.5)
    scores = (
        jnp.einsum("bhd,bld->bhl", rot_query, key_cache, preferred_element_type=jnp.float32) * scale
    )
    selfish = (
        jnp.einsum("bhd,bd->bh", rot_query, rot_key, preferred_element_type=jnp.float32) * scale
    )
    live = jnp.arange(key_cache.shape[1], dtype=jnp.int32)[None, :] < lengths[:, None]
    live = live[:, None, :]
    masked = jnp.where(live, scores, -1e30)
    peak = jnp.maximum(jnp.max(masked, -1), selfish)
    expo = jnp.where(live, jnp.exp(masked - peak[..., None]), 0.0)
    expo_self = jnp.exp(selfish - peak)
    total = jnp.sum(expo, -1) + expo_self
    probs = (expo / total[..., None]).astype(jnp.bfloat16)
    probs_self = (expo_self / total).astype(jnp.bfloat16)
    mixed = jnp.einsum("bhl,bld->bhd", probs, value_cache, preferred_element_type=jnp.float32)
    mixed = (
        mixed
        + probs_self.astype(jnp.float32)[..., None] * new_value.astype(jnp.float32)[:, None, :]
    )
    return mixed.reshape(count, heads_here * DH).astype(jnp.bfloat16)


def per_device(
    hidden_in, ln_gain, w_query, w_keyval, w_output, key_cache, value_cache, lengths, positions
):
    xf = hidden_in.astype(jnp.float32)
    totals, squares = lax.psum((jnp.sum(xf, 1), jnp.sum(xf * xf, 1)), "gx")
    mean = totals / D
    var = squares / D - mean * mean
    centered = xf - mean[:, None]
    normed = (centered * lax.rsqrt(var + 1e-05)[:, None] * ln_gain[None, :]).astype(jnp.bfloat16)
    all_rows = lax.all_gather(normed, ("gy", "gz"), axis=0, tiled=True)
    query_cols = w_query.shape[1]
    first = jnp.dot(all_rows, w_query, preferred_element_type=jnp.float32)
    second = jnp.dot(all_rows, w_keyval, preferred_element_type=jnp.float32)
    projected = lax.psum_scatter(
        jnp.concatenate([first, second], 1), "gx", scatter_dimension=0, tiled=True
    ).astype(jnp.bfloat16)
    query_part = projected[:, :query_cols]
    keyval_part = projected[:, query_cols:]
    query_seq, keyval_seq = (
        lax.all_to_all(query_part, ("gy", "gz"), split_axis=0, concat_axis=1, tiled=True),
        lax.all_to_all(keyval_part, ("gy", "gz"), split_axis=0, concat_axis=1, tiled=True),
    )
    attended = attend(query_seq, keyval_seq, key_cache, value_cache, lengths, positions)
    head_block = lax.all_to_all(attended, ("gy", "gz"), split_axis=1, concat_axis=0, tiled=True)
    partials = jnp.dot(
        lax.all_gather(head_block, "gx", axis=0, tiled=True),
        w_output,
        preferred_element_type=jnp.float32,
    )
    return lax.psum_scatter(
        partials.astype(jnp.bfloat16), ("gy", "gz"), scatter_dimension=0, tiled=True
    ).astype(jnp.float32)


def layer_kernel(
    sizes,
    x_ref, gain_ref, freq_ref, wq_hbm, wkv_hbm, wo_hbm, kc_hbm, vc_hbm, len_ref, pos_ref,
    out_ref,
    wq, wkv, wo, kc, vc,
    rows_x, stats, normed, q_send, q_recv, kv_send, kv_recv,
    h_send, h_recv, h_spread, h_rows, total, o_send, o_recv,
    load_sem, x_sem, stat_sem, kv_sem, q_sem, h_sem, o_sem,
):
    G, Y, Z = sizes
    C = Y * Z
    N = G * C
    H = CHUNK_HEADS
    chunks = wq.shape[0]
    count = 2 * C * G
    feats = x_ref.shape[1]
    half_feats = feats // 2
    out_chunks = o_send.shape[0]
    slots = kc.shape[0] // SEQS
    block = rows_x.shape[1] // 2
    gx, plane = lax.axis_index("gx"), lax.axis_index("gy") * Z + lax.axis_index("gz")
    me = gx * C + plane

    def device(rank):
        return {"gx": rank // C, "gy": rank % C // Z, "gz": rank % Z}

    def load(j, source, target):
        return pltpu.make_async_copy(source, target, load_sem.at[j])

    def arrived(ref, sem):
        pltpu.make_async_copy(ref, ref, sem).wait()

    def to_all(body):
        def step(k, carry):
            body(lax.rem(me + k, N))
            return carry

        lax.fori_loop(1, N, step, 0)

    loads = [load(0, wkv_hbm, wkv)]
    cols = H * DH
    for j in range(chunks):
        loads.append(load(1 + j, wq_hbm.at[:, pl.ds(j * cols, cols)], wq.at[j]))
    loads.append(load(1 + chunks, kc_hbm, kc))
    loads.append(load(2 + chunks, vc_hbm, vc))
    for j in range(chunks):
        loads.append(load(3 + chunks + j, wo_hbm.at[pl.ds(j * cols, cols), :], wo.at[j]))
    for j in range(1 + chunks):
        loads[j].start()

    barrier = pltpu.get_barrier_semaphore()

    def greet(rank):
        pl.semaphore_signal(barrier, inc=1, device_id=device(rank), device_id_type=MESH)

    to_all(greet)

    x = x_ref[...].astype(jnp.float32)
    folded = jnp.concatenate([x[:, :half_feats], x[:, half_feats:]], 0)
    rows_x[plane] = folded.astype(jnp.bfloat16)
    mean = jnp.sum(x, 1, keepdims=True) / feats
    centered = x - mean
    spread = jnp.sum(centered * centered, 1, keepdims=True)
    lane = lax.broadcasted_iota(jnp.int32, (block, LANES), 1)
    stats[me] = jnp.where(lane == 0, mean, spread)

    pl.semaphore_wait(barrier, N - 1)

    def send_rows(k, carry):
        rank = gx * C + lax.rem(plane + k, C)
        pltpu.make_async_remote_copy(
            src_ref=rows_x.at[plane], dst_ref=rows_x.at[plane],
            send_sem=x_sem.at[0], recv_sem=x_sem.at[1],
            device_id=device(rank), device_id_type=MESH,
        ).start()
        return carry

    lax.fori_loop(1, C, send_rows, 0)

    def send_stats(rank):
        pltpu.make_async_remote_copy(
            src_ref=stats.at[me], dst_ref=stats.at[me],
            send_sem=stat_sem.at[0], recv_sem=stat_sem.at[1],
            device_id=device(rank), device_id_type=MESH,
        ).start()

    to_all(send_stats)

    row = lax.broadcasted_iota(jnp.int32, (SEQS * H, LANES), 0)
    place = jnp.where(row < H, pos_ref[0], pos_ref[1]).astype(jnp.float32)
    angle = place * freq_ref[...]
    turns = jnp.floor(angle * (0.5 / math.pi) + 0.5)
    angle = angle - turns * 6.28125
    angle = angle - turns * (4058 / 2097152)
    angle = angle - turns * (2 * math.pi - 6.28125 - 4058 / 2097152)
    cosine, sine = jnp.cos(angle), jnp.sin(angle)

    def turned(t, cos, sin):
        t1, t2 = t[:, :HALF], t[:, HALF:]
        return jnp.concatenate([t1 * cos - t2 * sin, t2 * cos + t1 * sin], 1)

    cos_all = jnp.concatenate([cosine] * C, 0)
    sin_all = jnp.concatenate([sine] * C, 0)

    arrived(stats.at[pl.ds(0, N - 1)], stat_sem.at[1])
    arrived(rows_x.at[pl.ds(0, C - 1)], x_sem.at[1])

    for pair in range(C // 2):
        lows, highs = [], []
        for c in (2 * pair, 2 * pair + 1):
            parts = [stats[g * C + c] for g in range(G)]
            means = [p[:, 0:1] for p in parts]
            mean = functools.reduce(jnp.add, means) / G
            squares = functools.reduce(jnp.add, [p[:, 1:2] for p in parts])
            between = functools.reduce(jnp.add, [(m - mean) * (m - mean) for m in means])
            scale = lax.rsqrt((squares + feats * between) / (feats * G) + 1e-05)
            folded = rows_x[c].astype(jnp.float32)
            lows.append((folded[:block] - mean) * scale)
            highs.append((folded[block:] - mean) * scale)
        rows = pl.ds(2 * pair * block, 2 * block)
        low = jnp.concatenate(lows, 0) * gain_ref[:, :half_feats]
        high = jnp.concatenate(highs, 0) * gain_ref[:, half_feats:]
        normed[rows, pl.ds(0, half_feats)] = low.astype(jnp.bfloat16)
        normed[rows, pl.ds(half_feats, half_feats)] = high.astype(jnp.bfloat16)

    loads[0].wait()
    part = jnp.dot(normed[...], wkv[...], preferred_element_type=jnp.float32)
    for h in range(H):
        kv_send[pl.ds(h, count, stride=H), :] = part

    def send_kv(rank):
        pltpu.make_async_remote_copy(
            src_ref=kv_send.at[pl.ds(pl.multiple_of(rank * SEQS * H, SEQS * H), SEQS * H), :],
            dst_ref=kv_recv.at[me],
            send_sem=kv_sem.at[0], recv_sem=kv_sem.at[1],
            device_id=device(rank), device_id_type=MESH,
        ).start()

    to_all(send_kv)
    own = pl.ds(pl.multiple_of(me * SEQS * H, SEQS * H), SEQS * H)
    kv_recv[me] = kv_send[own, :]

    for j in range(chunks):
        loads[1 + j].wait()
        if j == 0:
            loads[1 + chunks].start()
            loads[2 + chunks].start()
        loads[3 + chunks + j].start()
        for h in range(0, H, 2):
            part = jnp.dot(
                normed[...], wq[j, :, h * DH:(h + 2) * DH], preferred_element_type=jnp.float32
            )
            for i in range(2):
                for side in range(2):
                    at = i * DH + side * HALF
                    q_send[j, side, pl.ds(h + i, count, stride=H), :] = part[:, at:at + HALF]

        def send_query(rank):
            rows = pl.ds(pl.multiple_of(rank * SEQS * H, SEQS * H), SEQS * H)
            pltpu.make_async_remote_copy(
                src_ref=q_send.at[j, :, rows, :], dst_ref=q_recv.at[j, me],
                send_sem=q_sem.at[0, j], recv_sem=q_sem.at[1, j],
                device_id=device(rank), device_id_type=MESH,
            ).start()

        to_all(send_query)
        q_recv[j, me] = q_send[j, :, own, :]

    arrived(kv_recv.at[pl.ds(0, N - 1)], kv_sem.at[1])
    pieces = []
    for c in range(C):
        pieces.append(functools.reduce(jnp.add, [kv_recv[g * C + c] for g in range(G)]))
    keyval = jnp.concatenate(pieces, 1).astype(jnp.bfloat16).astype(jnp.float32)
    rot_key = turned(keyval[:, :DH], cosine, sine).astype(jnp.bfloat16).astype(jnp.float32)
    key_all = jnp.concatenate([rot_key] * C, 0)
    value_all = jnp.concatenate([keyval[:, DH:]] * C, 0)

    loads[1 + chunks].wait()
    loads[2 + chunks].wait()
    rows_all = C * SEQS * H
    row = lax.broadcasted_iota(jnp.int32, (rows_all, SEQS * slots), 0)
    slot = lax.broadcasted_iota(jnp.int32, (rows_all, SEQS * slots), 1)
    second = lax.rem(row, SEQS * H) >= H
    base = jnp.where(second, slots, 0)
    live = (slot >= base) & (slot < base + jnp.where(second, len_ref[1], len_ref[0]))
    scale = DH ** (-0.5)

    for j in range(chunks):
        arrived(q_recv.at[j, pl.ds(0, N - 1)], q_sem.at[1, j])
        blocks = []
        for c in range(C):
            sides = []
            for side in range(2):
                sides.append(
                    functools.reduce(jnp.add, [q_recv[j, g * C + c, side] for g in range(G)])
                )
            blocks.append(jnp.concatenate(sides, 1))
        query = jnp.concatenate(blocks, 0).astype(jnp.bfloat16).astype(jnp.float32)
        rot_query = turned(query, cos_all, sin_all).astype(jnp.bfloat16)
        scores = lax.dot_general(
            rot_query, kc[...], (((1,), (1,)), ((), ())), preferred_element_type=jnp.float32
        ) * scale
        selfish = jnp.sum(rot_query.astype(jnp.float32) * key_all, 1, keepdims=True) * scale
        masked = jnp.where(live, scores, -1e30)
        peak = jnp.maximum(jnp.max(masked, 1, keepdims=True), selfish)
        expo = jnp.where(live, jnp.exp(masked - peak), 0.0)
        expo_self = jnp.exp(selfish - peak)
        denominator = jnp.sum(expo, 1, keepdims=True) + expo_self
        probs = (expo / denominator).astype(jnp.bfloat16)
        probs_self = (expo_self / denominator).astype(jnp.bfloat16).astype(jnp.float32)
        mixed = jnp.dot(probs, vc[...], preferred_element_type=jnp.float32)
        mixed = mixed + probs_self * value_all
        for c in range(C):
            tile = mixed[c * SEQS * H:(c + 1) * SEQS * H]
            h_send[j, c] = jnp.concatenate([tile[:, :HALF], tile[:, HALF:]], 0).astype(jnp.bfloat16)

        def send_heads(rank):
            pltpu.make_async_remote_copy(
                src_ref=h_send.at[j, rank % C], dst_ref=h_recv.at[j, me],
                send_sem=h_sem.at[0, j], recv_sem=h_sem.at[1, j],
                device_id=device(rank), device_id_type=MESH,
            ).start()

        to_all(send_heads)
        h_recv[j, me] = h_send[j, plane]

    def gather_heads(j):
        arrived(h_recv.at[j, pl.ds(0, N - 1)], h_sem.at[1, j])
        for rank in range(N):
            tile = h_recv[j, rank].astype(jnp.float32)
            for side in range(2):
                h_spread[side, rank * SEQS * H:(rank + 1) * SEQS * H] = tile[
                    side * SEQS * H:(side + 1) * SEQS * H
                ]
        for h in range(H):
            for side in range(2):
                at = h * DH + side * HALF
                h_rows[j, :, at:at + HALF] = h_spread[
                    side, pl.ds(h, count, stride=H), :
                ].astype(jnp.bfloat16)

    for j in range(chunks):
        gather_heads(j)
        loads[3 + chunks + j].wait()

        def columns(n, carry):
            at = pl.ds(pl.multiple_of(n * OUT_COLS, OUT_COLS), OUT_COLS)
            part = jnp.dot(h_rows[j], wo[j, :, at], preferred_element_type=jnp.float32)
            if j > 0:
                part = part + total[:, at]
            if j < chunks - 1:
                total[:, at] = part
                return carry
            for c in range(C):
                tile = part[c * block:(c + 1) * block]
                o_send[n, c] = jnp.concatenate(
                    [tile[:, :OUT_COLS // 2], tile[:, OUT_COLS // 2:]], 0
                ).astype(jnp.bfloat16)
            for k in range(1, C):
                other = lax.rem(plane + k, C)
                pltpu.make_async_remote_copy(
                    src_ref=o_send.at[n, other], dst_ref=o_recv.at[n, k - 1],
                    send_sem=o_sem.at[0, n], recv_sem=o_sem.at[1, n],
                    device_id=device(gx * C + other), device_id_type=MESH,
                ).start()
            return carry

        lax.fori_loop(0, out_chunks, columns, 0)

    def finish(n, carry):
        arrived(o_recv.at[n], o_sem.at[1, n])
        summed = o_send[n, plane].astype(jnp.float32)
        for k in range(C - 1):
            summed = summed + o_recv[n, k].astype(jnp.float32)
        low = pl.multiple_of(n * OUT_COLS, OUT_COLS // 2)
        high = pl.multiple_of(n * OUT_COLS + OUT_COLS // 2, OUT_COLS // 2)
        out_ref[:, pl.ds(low, OUT_COLS // 2)] = summed[:block]
        out_ref[:, pl.ds(high, OUT_COLS // 2)] = summed[block:]
        return carry

    lax.fori_loop(0, out_chunks, finish, 0)

    arrived(rows_x.at[pl.ds(0, C - 1)], x_sem.at[0])
    arrived(stats.at[pl.ds(0, N - 1)], stat_sem.at[0])
    arrived(kv_recv.at[pl.ds(0, N - 1)], kv_sem.at[0])
    for j in range(chunks):
        arrived(q_recv.at[j, pl.ds(0, N - 1)], q_sem.at[0, j])
        arrived(h_recv.at[j, pl.ds(0, N - 1)], h_sem.at[0, j])

    def left(n, carry):
        arrived(o_recv.at[n], o_sem.at[0, n])
        return carry

    lax.fori_loop(0, out_chunks, left, 0)


def fused(
    sizes, hidden_in, ln_gain, w_query, w_keyval, w_output, key_cache, value_cache, lengths, positions
):
    G, Y, Z = sizes
    C = Y * Z
    N = G * C
    block, feats = hidden_in.shape
    count = block * C
    H = CHUNK_HEADS
    chunks = w_query.shape[1] // (H * DH)
    out_cols = w_output.shape[1]
    out_chunks = out_cols // OUT_COLS
    keys = key_cache.reshape(-1, DH)
    values = value_cache.reshape(-1, DH)
    freqs = np.exp(-np.log(10000.0) * np.arange(HALF) / HALF).astype(np.float32)[None, :]
    bf16, f32 = jnp.bfloat16, jnp.float32
    vmem = pl.BlockSpec(memory_space=pltpu.VMEM)
    smem = pl.BlockSpec(memory_space=pltpu.SMEM)
    anywhere = pl.BlockSpec(memory_space=pl.ANY)
    tile = SEQS * H
    return pl.pallas_call(
        functools.partial(layer_kernel, sizes),
        out_shape=jax.ShapeDtypeStruct((block, out_cols), f32),
        in_specs=[vmem, vmem, vmem] + [anywhere] * 5 + [smem, smem],
        out_specs=vmem,
        scratch_shapes=[
            pltpu.VMEM((chunks, feats, H * DH), bf16),
            pltpu.VMEM(w_keyval.shape, bf16),
            pltpu.VMEM((chunks, H * DH, out_cols), bf16),
            pltpu.VMEM(keys.shape, bf16),
            pltpu.VMEM(values.shape, bf16),
            pltpu.VMEM((C, 2 * block, feats // 2), bf16),
            pltpu.VMEM((N, block, LANES), f32),
            pltpu.VMEM((count, feats), bf16),
            pltpu.VMEM((chunks, 2, N * tile, HALF), f32),
            pltpu.VMEM((chunks, N, 2, tile, HALF), f32),
            pltpu.VMEM((N * tile, w_keyval.shape[1]), f32),
            pltpu.VMEM((N, tile, w_keyval.shape[1]), f32),
            pltpu.VMEM((chunks, C, 2 * tile, HALF), bf16),
            pltpu.VMEM((chunks, N, 2 * tile, HALF), bf16),
            pltpu.VMEM((2, N * tile, HALF), f32),
            pltpu.VMEM((chunks, count, H * DH), bf16),
            pltpu.VMEM((count, out_cols), f32),
            pltpu.VMEM((out_chunks, C, 2 * block, OUT_COLS // 2), bf16),
            pltpu.VMEM((out_chunks, C - 1, 2 * block, OUT_COLS // 2), bf16),
            pltpu.SemaphoreType.DMA((3 + 2 * chunks,)),
            pltpu.SemaphoreType.DMA((2,)),
            pltpu.SemaphoreType.DMA((2,)),
            pltpu.SemaphoreType.DMA((2,)),
            pltpu.SemaphoreType.DMA((2, chunks)),
            pltpu.SemaphoreType.DMA((2, chunks)),
            pltpu.SemaphoreType.DMA((2, out_chunks)),
        ],
        compiler_params=pltpu.CompilerParams(
            collective_id=0, has_side_effects=True, vmem_limit_bytes=62 * 1024 * 1024
        ),
    )(
        hidden_in, ln_gain.reshape(1, -1), jnp.asarray(freqs), w_query, w_keyval, w_output,
        keys, values, lengths, positions,
    )


def solution(mesh):
    sizes = (mesh.shape["gx"], mesh.shape["gy"], mesh.shape["gz"])
    plane = sizes[1] * sizes[2]

    def layer(*args):
        hidden_in, _, w_query, w_keyval, w_output, key_cache = args[:6]
        fits = (
            key_cache.shape[0] == SEQS
            and hidden_in.shape[0] == 8
            and plane % 2 == 0
            and hidden_in.shape[1] % (2 * LANES) == 0
            and w_query.shape[1] % (CHUNK_HEADS * DH) == 0
            and w_keyval.shape[1] == LANES
            and w_output.shape[1] % OUT_COLS == 0
        )
        if fits:
            return fused(sizes, *args)
        return per_device(*args)

    in_specs = (
        P(("grp", "gy", "gz"), "gx"),
        P("gx"),
        P("gx", ("gy", "gz")),
        P("gx", ("gy", "gz")),
        P(("gy", "gz"), "gx"),
        P(("grp", "gx", "gy", "gz"), None, None),
        P(("grp", "gx", "gy", "gz"), None, None),
        P(("grp", "gx", "gy", "gz")),
        P(("grp", "gx", "gy", "gz")),
    )
    out_specs = P(("grp", "gy", "gz"), "gx")
    return jax.shard_map(layer, mesh=mesh, in_specs=in_specs, out_specs=out_specs, check_vma=False)
```

```python
import functools
import math

import jax
import jax.numpy as jnp
import numpy as np
from jax import lax
from jax.experimental import pallas as pl
from jax.experimental.pallas import tpu as pltpu
from jax.sharding import PartitionSpec as P

D = 18432
DH = 256
HALF = DH // 2
LANES = 128
MESH = pl.DeviceIdType.MESH
CHUNK_HEADS = 4
OUT_COLS = 768
SEQS = 2


def rotary(values, places):
    half = values.shape[-1] // 2
    freqs = jnp.exp(-jnp.log(10000.0) * jnp.arange(half, dtype=jnp.float32) / half)
    angles = places.astype(jnp.float32)[:, None] * freqs[None, :]
    while angles.ndim < values.ndim:
        angles = angles[:, None, :]
    cosine = jnp.cos(angles)
    sine = jnp.sin(angles)
    first = values[..., :half]
    second = values[..., half:]
    return jnp.concatenate([first * cosine - second * sine, second * cosine + first * sine], -1)


def attend(query2d, keyval2d, key_cache, value_cache, lengths, positions):
    count = query2d.shape[0]
    heads_here = query2d.shape[1] // DH
    query = query2d.reshape(count, heads_here, DH).astype(jnp.float32)
    rot_query = rotary(query, positions).astype(jnp.bfloat16)
    rot_key = rotary(keyval2d[:, :DH].astype(jnp.float32), positions).astype(jnp.bfloat16)
    new_value = keyval2d[:, DH:]
    scale = DH ** (-0.5)
    scores = (
        jnp.einsum("bhd,bld->bhl", rot_query, key_cache, preferred_element_type=jnp.float32) * scale
    )
    selfish = (
        jnp.einsum("bhd,bd->bh", rot_query, rot_key, preferred_element_type=jnp.float32) * scale
    )
    live = jnp.arange(key_cache.shape[1], dtype=jnp.int32)[None, :] < lengths[:, None]
    live = live[:, None, :]
    masked = jnp.where(live, scores, -1e30)
    peak = jnp.maximum(jnp.max(masked, -1), selfish)
    expo = jnp.where(live, jnp.exp(masked - peak[..., None]), 0.0)
    expo_self = jnp.exp(selfish - peak)
    total = jnp.sum(expo, -1) + expo_self
    probs = (expo / total[..., None]).astype(jnp.bfloat16)
    probs_self = (expo_self / total).astype(jnp.bfloat16)
    mixed = jnp.einsum("bhl,bld->bhd", probs, value_cache, preferred_element_type=jnp.float32)
    mixed = (
        mixed
        + probs_self.astype(jnp.float32)[..., None] * new_value.astype(jnp.float32)[:, None, :]
    )
    return mixed.reshape(count, heads_here * DH).astype(jnp.bfloat16)


def per_device(
    hidden_in, ln_gain, w_query, w_keyval, w_output, key_cache, value_cache, lengths, positions
):
    xf = hidden_in.astype(jnp.float32)
    totals, squares = lax.psum((jnp.sum(xf, 1), jnp.sum(xf * xf, 1)), "gx")
    mean = totals / D
    var = squares / D - mean * mean
    centered = xf - mean[:, None]
    normed = (centered * lax.rsqrt(var + 1e-05)[:, None] * ln_gain[None, :]).astype(jnp.bfloat16)
    all_rows = lax.all_gather(normed, ("gy", "gz"), axis=0, tiled=True)
    query_cols = w_query.shape[1]
    first = jnp.dot(all_rows, w_query, preferred_element_type=jnp.float32)
    second = jnp.dot(all_rows, w_keyval, preferred_element_type=jnp.float32)
    projected = lax.psum_scatter(
        jnp.concatenate([first, second], 1), "gx", scatter_dimension=0, tiled=True
    ).astype(jnp.bfloat16)
    query_part = projected[:, :query_cols]
    keyval_part = projected[:, query_cols:]
    query_seq, keyval_seq = (
        lax.all_to_all(query_part, ("gy", "gz"), split_axis=0, concat_axis=1, tiled=True),
        lax.all_to_all(keyval_part, ("gy", "gz"), split_axis=0, concat_axis=1, tiled=True),
    )
    attended = attend(query_seq, keyval_seq, key_cache, value_cache, lengths, positions)
    head_block = lax.all_to_all(attended, ("gy", "gz"), split_axis=1, concat_axis=0, tiled=True)
    partials = jnp.dot(
        lax.all_gather(head_block, "gx", axis=0, tiled=True),
        w_output,
        preferred_element_type=jnp.float32,
    )
    return lax.psum_scatter(
        partials.astype(jnp.bfloat16), ("gy", "gz"), scatter_dimension=0, tiled=True
    ).astype(jnp.float32)


def layer_kernel(
    sizes,
    x_hbm, gain_hbm, freq_hbm, wq_hbm, wkv_hbm, wo_hbm, kc_hbm, vc_hbm, len_hbm, pos_hbm,
    out_ref,
    x_ref, gain_ref, freq_ref, len_ref, pos_ref,
    wq, wkv, wo, kc, vc,
    rows_x, stats, normed, q_send, q_recv, kv_send, kv_recv,
    h_send, h_recv, spread, h_rows, total, o_send, o_recv,
    small_sem, load_sem, x_sem, stat_sem, kv_sem, q_sem, h_sem, o_sem,
):
    G, Y, Z = sizes
    C = Y * Z
    N = G * C
    H = CHUNK_HEADS
    chunks = wq.shape[0]
    count = 2 * C * G
    feats = x_ref.shape[1]
    half_feats = feats // 2
    quarter = feats // 4
    out_chunks = o_send.shape[0]
    slots = kc.shape[0] // SEQS
    block = x_ref.shape[0]
    gx, gy, gz = (lax.axis_index(axis) for axis in ("gx", "gy", "gz"))
    plane = gy * Z + gz
    me = gx * C + plane

    def device(rank):
        return {"gx": rank // C, "gy": rank % C // Z, "gz": rank % Z}

    def load(j, source, target):
        return pltpu.make_async_copy(source, target, load_sem.at[j])

    def arrived(ref, sem):
        pltpu.make_async_copy(ref, ref, sem).wait()

    def to_all(body):
        def step(k, carry):
            body(lax.rem(me + k, N))
            return carry

        lax.fori_loop(1, N, step, 0)

    barrier = pltpu.get_barrier_semaphore()

    def greet(rank):
        pl.semaphore_signal(barrier, inc=1, device_id=device(rank), device_id_type=MESH)

    to_all(greet)

    smalls = [
        pltpu.make_async_copy(source, target, small_sem.at[i])
        for i, (source, target) in enumerate(
            [(x_hbm, x_ref), (gain_hbm, gain_ref), (freq_hbm, freq_ref),
             (len_hbm, len_ref), (pos_hbm, pos_ref)]
        )
    ]
    for copy in smalls:
        copy.start()
    loads = [load(0, wkv_hbm, wkv)]
    cols = H * DH
    for j in range(chunks):
        loads.append(load(1 + j, wq_hbm.at[:, pl.ds(j * cols, cols)], wq.at[j]))
    loads.append(load(1 + chunks, kc_hbm, kc))
    loads.append(load(2 + chunks, vc_hbm, vc))
    for j in range(chunks):
        loads.append(load(3 + chunks + j, wo_hbm.at[pl.ds(j * cols, cols), :], wo.at[j]))
    for j in range(1 + chunks):
        loads[j].start()

    smalls[0].wait()
    x = x_ref[...].astype(jnp.float32)
    for half in range(2):
        at = half * half_feats
        folded = jnp.concatenate([x[:, at:at + quarter], x[:, at + quarter:at + half_feats]], 0)
        rows_x[half, plane] = folded.astype(jnp.bfloat16)
    mean = jnp.sum(x, 1, keepdims=True) / feats
    centered = x - mean
    squares = jnp.sum(centered * centered, 1, keepdims=True)
    lane = lax.broadcasted_iota(jnp.int32, (block, LANES), 1)
    stats[me] = jnp.where(lane == 0, mean, squares)

    pl.semaphore_wait(barrier, N - 1)

    def send_rows(half):
        for k in range(1, C):
            pltpu.make_async_remote_copy(
                src_ref=rows_x.at[half, plane], dst_ref=rows_x.at[half, plane],
                send_sem=x_sem.at[0, half], recv_sem=x_sem.at[1, half],
                device_id=device(gx * C + lax.rem(plane + k, C)), device_id_type=MESH,
            ).start()

    send_rows(0)

    def send_stats(rank):
        pltpu.make_async_remote_copy(
            src_ref=stats.at[me], dst_ref=stats.at[me],
            send_sem=stat_sem.at[0], recv_sem=stat_sem.at[1],
            device_id=device(rank), device_id_type=MESH,
        ).start()

    to_all(send_stats)
    send_rows(1)

    for copy in smalls[1:]:
        copy.wait()

    row = lax.broadcasted_iota(jnp.int32, (SEQS * H, LANES), 0)
    place = jnp.where(row < H, pos_ref[0], pos_ref[1]).astype(jnp.float32)
    angle = place * freq_ref[...]
    turns = jnp.floor(angle * (0.5 / math.pi) + 0.5)
    angle = angle - turns * 6.28125
    angle = angle - turns * (4058 / 2097152)
    angle = angle - turns * (2 * math.pi - 6.28125 - 4058 / 2097152)
    cosine, sine = jnp.cos(angle), jnp.sin(angle)

    def turned(t, cos, sin):
        t1, t2 = t[:, :HALF], t[:, HALF:]
        return jnp.concatenate([t1 * cos - t2 * sin, t2 * cos + t1 * sin], 1)

    cos_all = jnp.concatenate([cosine] * C, 0)
    sin_all = jnp.concatenate([sine] * C, 0)

    arrived(stats.at[pl.ds(0, N - 1)], stat_sem.at[1])
    moments = []
    for c in range(C):
        parts = [stats[g * C + c] for g in range(G)]
        means = [p[:, 0:1] for p in parts]
        mean = functools.reduce(jnp.add, means) / G
        squares = functools.reduce(jnp.add, [p[:, 1:2] for p in parts])
        between = functools.reduce(jnp.add, [(m - mean) * (m - mean) for m in means])
        moments.append((mean, lax.rsqrt((squares + feats * between) / (feats * G) + 1e-05)))

    def normalize(half):
        arrived(rows_x.at[half, pl.ds(0, C - 1)], x_sem.at[1, half])
        for pair in range(C // 2):
            lows, highs = [], []
            for c in (2 * pair, 2 * pair + 1):
                mean, scale = moments[c]
                folded = rows_x[half, c].astype(jnp.float32)
                lows.append((folded[:block] - mean) * scale)
                highs.append((folded[block:] - mean) * scale)
            rows = pl.ds(2 * pair * block, 2 * block)
            for at, part in ((half * half_feats, lows), (half * half_feats + quarter, highs)):
                part = jnp.concatenate(part, 0) * gain_ref[pl.ds(at, quarter)][None, :]
                normed[rows, pl.ds(at, quarter)] = part.astype(jnp.bfloat16)

    normalize(0)
    loads[1].wait()
    for h in range(0, H, 2):
        at = slice(h * DH, (h + 2) * DH)
        total[:, at] = jnp.dot(
            normed[:, :half_feats], wq[0, :half_feats, at], preferred_element_type=jnp.float32
        )
    normalize(1)

    loads[0].wait()
    part = jnp.dot(normed[...], wkv[...], preferred_element_type=jnp.float32)
    for rank in range(N):
        kv_send[rank] = part[rank * SEQS:(rank + 1) * SEQS]

    def send_kv(rank):
        pltpu.make_async_remote_copy(
            src_ref=kv_send.at[rank], dst_ref=kv_recv.at[me],
            send_sem=kv_sem.at[0], recv_sem=kv_sem.at[1],
            device_id=device(rank), device_id_type=MESH,
        ).start()

    to_all(send_kv)
    kv_recv[me] = kv_send[me]

    for j in range(chunks):
        if j > 0:
            loads[1 + j].wait()
        if j == 0:
            loads[1 + chunks].start()
            loads[2 + chunks].start()
        loads[3 + chunks + j].start()
        for h in range(0, H, 2):
            at = slice(h * DH, (h + 2) * DH)
            if j == 0:
                part = total[:, at] + jnp.dot(
                    normed[:, half_feats:], wq[j, half_feats:, at],
                    preferred_element_type=jnp.float32,
                )
            else:
                part = jnp.dot(normed[...], wq[j, :, at], preferred_element_type=jnp.float32)
            for i in range(2):
                for side in range(2):
                    at = i * DH + side * HALF
                    spread[side, pl.ds(h + i, count, stride=H), :] = part[:, at:at + HALF]
        tiles = [spread[side].reshape(N, SEQS * H, HALF) for side in range(2)]
        q_send[j] = jnp.concatenate(tiles, 1)

        def send_query(rank):
            pltpu.make_async_remote_copy(
                src_ref=q_send.at[j, rank], dst_ref=q_recv.at[j, me],
                send_sem=q_sem.at[0, j], recv_sem=q_sem.at[1, j],
                device_id=device(rank), device_id_type=MESH,
            ).start()

        to_all(send_query)
        q_recv[j, me] = q_send[j, me]

    arrived(kv_recv.at[pl.ds(0, N - 1)], kv_sem.at[1])
    pieces = []
    for c in range(C):
        pieces.append(functools.reduce(jnp.add, [kv_recv[g * C + c] for g in range(G)]))
    keyval = jnp.concatenate(pieces, 1)
    keyval = jnp.concatenate(
        [jnp.broadcast_to(keyval[i:i + 1], (H, 2 * DH)) for i in range(SEQS)], 0
    )
    keyval = keyval.astype(jnp.bfloat16).astype(jnp.float32)
    rot_key = turned(keyval[:, :DH], cosine, sine).astype(jnp.bfloat16).astype(jnp.float32)
    key_all = jnp.concatenate([rot_key] * C, 0)
    value_all = jnp.concatenate([keyval[:, DH:]] * C, 0)

    loads[1 + chunks].wait()
    loads[2 + chunks].wait()
    rows_all = C * SEQS * H
    row = lax.broadcasted_iota(jnp.int32, (rows_all, SEQS * slots), 0)
    slot = lax.broadcasted_iota(jnp.int32, (rows_all, SEQS * slots), 1)
    second = lax.rem(row, SEQS * H) >= H
    base = jnp.where(second, slots, 0)
    live = (slot >= base) & (slot < base + jnp.where(second, len_ref[1], len_ref[0]))
    scale = DH ** (-0.5)

    for j in range(chunks):
        arrived(q_recv.at[j, pl.ds(0, N - 1)], q_sem.at[1, j])
        blocks = []
        for c in range(C):
            tile = functools.reduce(jnp.add, [q_recv[j, g * C + c] for g in range(G)])
            blocks.append(jnp.concatenate([tile[:SEQS * H], tile[SEQS * H:]], 1))
        query = jnp.concatenate(blocks, 0).astype(jnp.bfloat16).astype(jnp.float32)
        rot_query = turned(query, cos_all, sin_all).astype(jnp.bfloat16)
        scores = lax.dot_general(
            rot_query, kc[...], (((1,), (1,)), ((), ())), preferred_element_type=jnp.float32
        ) * scale
        selfish = jnp.sum(rot_query.astype(jnp.float32) * key_all, 1, keepdims=True) * scale
        masked = jnp.where(live, scores, -1e30)
        peak = jnp.maximum(jnp.max(masked, 1, keepdims=True), selfish)
        expo = jnp.where(live, jnp.exp(masked - peak), 0.0)
        expo_self = jnp.exp(selfish - peak)
        denominator = jnp.sum(expo, 1, keepdims=True) + expo_self
        probs = (expo / denominator).astype(jnp.bfloat16)
        probs_self = (expo_self / denominator).astype(jnp.bfloat16).astype(jnp.float32)
        mixed = jnp.dot(probs, vc[...], preferred_element_type=jnp.float32)
        mixed = mixed + probs_self * value_all
        for c in range(C):
            tile = mixed[c * SEQS * H:(c + 1) * SEQS * H]
            h_send[j, c] = jnp.concatenate([tile[:, :HALF], tile[:, HALF:]], 0).astype(jnp.bfloat16)

        def send_heads(rank):
            pltpu.make_async_remote_copy(
                src_ref=h_send.at[j, rank % C], dst_ref=h_recv.at[j, me],
                send_sem=h_sem.at[0, j], recv_sem=h_sem.at[1, j],
                device_id=device(rank), device_id_type=MESH,
            ).start()

        to_all(send_heads)
        h_recv[j, me] = h_send[j, plane]

    def gather_heads(j):
        arrived(h_recv.at[j, pl.ds(0, N - 1)], h_sem.at[1, j])
        for rank in range(N):
            tile = h_recv[j, rank].astype(jnp.float32)
            for side in range(2):
                spread[side, rank * SEQS * H:(rank + 1) * SEQS * H] = tile[
                    side * SEQS * H:(side + 1) * SEQS * H
                ]
        for h in range(H):
            for side in range(2):
                at = h * DH + side * HALF
                h_rows[j, :, at:at + HALF] = spread[
                    side, pl.ds(h, count, stride=H), :
                ].astype(jnp.bfloat16)

    for j in range(chunks):
        gather_heads(j)
        loads[3 + chunks + j].wait()

        def columns(n, carry):
            at = pl.ds(pl.multiple_of(n * OUT_COLS, OUT_COLS), OUT_COLS)
            part = jnp.dot(h_rows[j], wo[j, :, at], preferred_element_type=jnp.float32)
            if j > 0:
                part = part + total[:, at]
            if j < chunks - 1:
                total[:, at] = part
                return carry
            for c in range(C):
                tile = part[c * block:(c + 1) * block]
                o_send[n, c] = jnp.concatenate(
                    [tile[:, :OUT_COLS // 2], tile[:, OUT_COLS // 2:]], 0
                ).astype(jnp.bfloat16)
            for k in range(1, C):
                other = lax.rem(plane + k, C)
                pltpu.make_async_remote_copy(
                    src_ref=o_send.at[n, other], dst_ref=o_recv.at[n, k - 1],
                    send_sem=o_sem.at[0, n], recv_sem=o_sem.at[1, n],
                    device_id=device(gx * C + other), device_id_type=MESH,
                ).start()
            return carry

        lax.fori_loop(0, out_chunks, columns, 0)

    def finish(n, carry):
        arrived(o_recv.at[n], o_sem.at[1, n])
        summed = o_send[n, plane].astype(jnp.float32)
        for k in range(C - 1):
            summed = summed + o_recv[n, k].astype(jnp.float32)
        low = pl.multiple_of(n * OUT_COLS, OUT_COLS // 2)
        high = pl.multiple_of(n * OUT_COLS + OUT_COLS // 2, OUT_COLS // 2)
        out_ref[:, pl.ds(low, OUT_COLS // 2)] = summed[:block]
        out_ref[:, pl.ds(high, OUT_COLS // 2)] = summed[block:]
        return carry

    lax.fori_loop(0, out_chunks, finish, 0)

    for half in range(2):
        arrived(rows_x.at[half, pl.ds(0, C - 1)], x_sem.at[0, half])
    arrived(stats.at[pl.ds(0, N - 1)], stat_sem.at[0])
    arrived(kv_recv.at[pl.ds(0, N - 1)], kv_sem.at[0])
    for j in range(chunks):
        arrived(q_recv.at[j, pl.ds(0, N - 1)], q_sem.at[0, j])
        arrived(h_recv.at[j, pl.ds(0, N - 1)], h_sem.at[0, j])

    def left(n, carry):
        arrived(o_recv.at[n], o_sem.at[0, n])
        return carry

    lax.fori_loop(0, out_chunks, left, 0)


def fused(
    sizes, hidden_in, ln_gain, w_query, w_keyval, w_output, key_cache, value_cache, lengths, positions
):
    G, Y, Z = sizes
    C = Y * Z
    N = G * C
    block, feats = hidden_in.shape
    count = block * C
    H = CHUNK_HEADS
    chunks = w_query.shape[1] // (H * DH)
    out_cols = w_output.shape[1]
    out_chunks = out_cols // OUT_COLS
    keys = key_cache.reshape(-1, DH)
    values = value_cache.reshape(-1, DH)
    freqs = np.exp(-np.log(10000.0) * np.arange(HALF) / HALF).astype(np.float32)[None, :]
    bf16, f32 = jnp.bfloat16, jnp.float32
    vmem = pl.BlockSpec(memory_space=pltpu.VMEM)
    anywhere = pl.BlockSpec(memory_space=pl.ANY)
    tile = SEQS * H
    return pl.pallas_call(
        functools.partial(layer_kernel, sizes),
        out_shape=pltpu.VMEM((block, out_cols), f32),
        in_specs=[anywhere] * 10,
        out_specs=vmem,
        scratch_shapes=[
            pltpu.VMEM(hidden_in.shape, bf16),
            pltpu.VMEM(ln_gain.shape, f32),
            pltpu.VMEM(freqs.shape, f32),
            pltpu.SMEM(lengths.shape, jnp.int32),
            pltpu.SMEM(positions.shape, jnp.int32),
            pltpu.VMEM((chunks, feats, H * DH), bf16),
            pltpu.VMEM(w_keyval.shape, bf16),
            pltpu.VMEM((chunks, H * DH, out_cols), bf16),
            pltpu.VMEM(keys.shape, bf16),
            pltpu.VMEM(values.shape, bf16),
            pltpu.VMEM((2, C, 2 * block, feats // 4), bf16),
            pltpu.VMEM((N, block, LANES), f32),
            pltpu.VMEM((count, feats), bf16),
            pltpu.VMEM((chunks, N, 2 * tile, HALF), f32),
            pltpu.VMEM((chunks, N, 2 * tile, HALF), f32),
            pltpu.VMEM((N, SEQS, w_keyval.shape[1]), f32),
            pltpu.VMEM((N, SEQS, w_keyval.shape[1]), f32),
            pltpu.VMEM((chunks, C, 2 * tile, HALF), bf16),
            pltpu.VMEM((chunks, N, 2 * tile, HALF), bf16),
            pltpu.VMEM((2, N * tile, HALF), f32),
            pltpu.VMEM((chunks, count, H * DH), bf16),
            pltpu.VMEM((count, out_cols), f32),
            pltpu.VMEM((out_chunks, C, 2 * block, OUT_COLS // 2), bf16),
            pltpu.VMEM((out_chunks, C - 1, 2 * block, OUT_COLS // 2), bf16),
            pltpu.SemaphoreType.DMA((5,)),
            pltpu.SemaphoreType.DMA((3 + 2 * chunks,)),
            pltpu.SemaphoreType.DMA((2, 2)),
            pltpu.SemaphoreType.DMA((2,)),
            pltpu.SemaphoreType.DMA((2,)),
            pltpu.SemaphoreType.DMA((2, chunks)),
            pltpu.SemaphoreType.DMA((2, chunks)),
            pltpu.SemaphoreType.DMA((2, out_chunks)),
        ],
        compiler_params=pltpu.CompilerParams(
            collective_id=0, has_side_effects=True, vmem_limit_bytes=62 * 1024 * 1024
        ),
    )(
        hidden_in, ln_gain, jnp.asarray(freqs), w_query, w_keyval, w_output,
        keys, values, lengths, positions,
    )


def solution(mesh):
    sizes = (mesh.shape["gx"], mesh.shape["gy"], mesh.shape["gz"])

    def layer(*args):
        hidden_in, _, w_query, w_keyval, w_output, key_cache = args[:6]
        fits = (
            key_cache.shape[0] == SEQS
            and hidden_in.shape[0] == 8
            and sizes[1] * sizes[2] % 2 == 0
            and w_keyval.shape[1] * sizes[1] * sizes[2] == 2 * DH
            and hidden_in.shape[1] % (4 * LANES) == 0
            and w_query.shape[1] % (CHUNK_HEADS * DH) == 0
            and w_keyval.shape[1] == LANES
            and w_output.shape[1] % OUT_COLS == 0
        )
        if fits:
            return fused(sizes, *args)
        return per_device(*args)

    in_specs = (
        P(("grp", "gy", "gz"), "gx"),
        P("gx"),
        P("gx", ("gy", "gz")),
        P("gx", ("gy", "gz")),
        P(("gy", "gz"), "gx"),
        P(("grp", "gx", "gy", "gz"), None, None),
        P(("grp", "gx", "gy", "gz"), None, None),
        P(("grp", "gx", "gy", "gz")),
        P(("grp", "gx", "gy", "gz")),
    )
    out_specs = P(("grp", "gy", "gz"), "gx")
    return jax.shard_map(layer, mesh=mesh, in_specs=in_specs, out_specs=out_specs, check_vma=False)
```

```python
import functools
import math

import jax
import jax.numpy as jnp
import numpy as np
from jax import lax
from jax.experimental import pallas as pl
from jax.experimental.pallas import tpu as pltpu
from jax.sharding import PartitionSpec as P

D = 18432
DH = 256
HALF = DH // 2
LANES = 128
MESH = pl.DeviceIdType.MESH
CHUNK_HEADS = 4
OUT_COLS = 1536
SEQS = 2


def rotary(values, places):
    half = values.shape[-1] // 2
    freqs = jnp.exp(-jnp.log(10000.0) * jnp.arange(half, dtype=jnp.float32) / half)
    angles = places.astype(jnp.float32)[:, None] * freqs[None, :]
    while angles.ndim < values.ndim:
        angles = angles[:, None, :]
    cosine = jnp.cos(angles)
    sine = jnp.sin(angles)
    first = values[..., :half]
    second = values[..., half:]
    return jnp.concatenate([first * cosine - second * sine, second * cosine + first * sine], -1)


def attend(query2d, keyval2d, key_cache, value_cache, lengths, positions):
    count = query2d.shape[0]
    heads_here = query2d.shape[1] // DH
    query = query2d.reshape(count, heads_here, DH).astype(jnp.float32)
    rot_query = rotary(query, positions).astype(jnp.bfloat16)
    rot_key = rotary(keyval2d[:, :DH].astype(jnp.float32), positions).astype(jnp.bfloat16)
    new_value = keyval2d[:, DH:]
    scale = DH ** (-0.5)
    scores = (
        jnp.einsum("bhd,bld->bhl", rot_query, key_cache, preferred_element_type=jnp.float32) * scale
    )
    selfish = (
        jnp.einsum("bhd,bd->bh", rot_query, rot_key, preferred_element_type=jnp.float32) * scale
    )
    live = jnp.arange(key_cache.shape[1], dtype=jnp.int32)[None, :] < lengths[:, None]
    live = live[:, None, :]
    masked = jnp.where(live, scores, -1e30)
    peak = jnp.maximum(jnp.max(masked, -1), selfish)
    expo = jnp.where(live, jnp.exp(masked - peak[..., None]), 0.0)
    expo_self = jnp.exp(selfish - peak)
    total = jnp.sum(expo, -1) + expo_self
    probs = (expo / total[..., None]).astype(jnp.bfloat16)
    probs_self = (expo_self / total).astype(jnp.bfloat16)
    mixed = jnp.einsum("bhl,bld->bhd", probs, value_cache, preferred_element_type=jnp.float32)
    mixed = (
        mixed
        + probs_self.astype(jnp.float32)[..., None] * new_value.astype(jnp.float32)[:, None, :]
    )
    return mixed.reshape(count, heads_here * DH).astype(jnp.bfloat16)


def per_device(
    hidden_in, ln_gain, w_query, w_keyval, w_output, key_cache, value_cache, lengths, positions
):
    xf = hidden_in.astype(jnp.float32)
    totals, squares = lax.psum((jnp.sum(xf, 1), jnp.sum(xf * xf, 1)), "gx")
    mean = totals / D
    var = squares / D - mean * mean
    centered = xf - mean[:, None]
    normed = (centered * lax.rsqrt(var + 1e-05)[:, None] * ln_gain[None, :]).astype(jnp.bfloat16)
    all_rows = lax.all_gather(normed, ("gy", "gz"), axis=0, tiled=True)
    query_cols = w_query.shape[1]
    first = jnp.dot(all_rows, w_query, preferred_element_type=jnp.float32)
    second = jnp.dot(all_rows, w_keyval, preferred_element_type=jnp.float32)
    projected = lax.psum_scatter(
        jnp.concatenate([first, second], 1), "gx", scatter_dimension=0, tiled=True
    ).astype(jnp.bfloat16)
    query_part = projected[:, :query_cols]
    keyval_part = projected[:, query_cols:]
    query_seq, keyval_seq = (
        lax.all_to_all(query_part, ("gy", "gz"), split_axis=0, concat_axis=1, tiled=True),
        lax.all_to_all(keyval_part, ("gy", "gz"), split_axis=0, concat_axis=1, tiled=True),
    )
    attended = attend(query_seq, keyval_seq, key_cache, value_cache, lengths, positions)
    head_block = lax.all_to_all(attended, ("gy", "gz"), split_axis=1, concat_axis=0, tiled=True)
    partials = jnp.dot(
        lax.all_gather(head_block, "gx", axis=0, tiled=True),
        w_output,
        preferred_element_type=jnp.float32,
    )
    return lax.psum_scatter(
        partials.astype(jnp.bfloat16), ("gy", "gz"), scatter_dimension=0, tiled=True
    ).astype(jnp.float32)


def layer_kernel(
    sizes,
    x_hbm, gain_hbm, freq_hbm, wq_hbm, wkv_hbm, wo_hbm, kc_hbm, vc_hbm, len_hbm, pos_hbm,
    out_ref,
    x_ref, gain_ref, freq_ref, len_ref, pos_ref,
    wq, wkv, wo, kc, vc,
    rows_x, stats, normed, q_send, q_recv, kv_send, kv_recv,
    h_send, h_recv, spread, h_rows, total, o_send, o_recv,
    small_sem, load_sem, x_sem, stat_sem, kv_sem, q_sem, h_sem, o_sem,
):
    G, Y, Z = sizes
    C = Y * Z
    N = G * C
    H = CHUNK_HEADS
    chunks = wq.shape[0]
    count = 2 * C * G
    feats = x_ref.shape[1]
    half_feats = feats // 2
    quarter = feats // 4
    out_chunks = o_send.shape[0]
    slots = kc.shape[0] // SEQS
    block = x_ref.shape[0]
    gx, gy, gz = (lax.axis_index(axis) for axis in ("gx", "gy", "gz"))
    plane = gy * Z + gz
    me = gx * C + plane

    def device(rank):
        return {"gx": rank // C, "gy": rank % C // Z, "gz": rank % Z}

    def load(j, source, target):
        return pltpu.make_async_copy(source, target, load_sem.at[j])

    def arrived(ref, sem):
        pltpu.make_async_copy(ref, ref, sem).wait()

    def to_all(body):
        def step(k, carry):
            body(lax.rem(me + k, N))
            return carry

        lax.fori_loop(1, N, step, 0)

    barrier = pltpu.get_barrier_semaphore()

    def greet(rank):
        pl.semaphore_signal(barrier, inc=1, device_id=device(rank), device_id_type=MESH)

    to_all(greet)

    smalls = [
        pltpu.make_async_copy(source, target, small_sem.at[i])
        for i, (source, target) in enumerate(
            [(x_hbm, x_ref), (gain_hbm, gain_ref), (freq_hbm, freq_ref),
             (len_hbm, len_ref), (pos_hbm, pos_ref)]
        )
    ]
    for copy in smalls:
        copy.start()
    loads = [load(0, wkv_hbm, wkv)]
    cols = H * DH
    for j in range(chunks):
        loads.append(load(1 + j, wq_hbm.at[:, pl.ds(j * cols, cols)], wq.at[j]))
    loads.append(load(1 + chunks, kc_hbm, kc))
    loads.append(load(2 + chunks, vc_hbm, vc))
    for j in range(chunks):
        loads.append(load(3 + chunks + j, wo_hbm.at[pl.ds(j * cols, cols), :], wo.at[j]))
    for j in range(1 + chunks):
        loads[j].start()

    smalls[0].wait()
    x = x_ref[...].astype(jnp.float32)
    for half in range(2):
        at = half * half_feats
        folded = jnp.concatenate([x[:, at:at + quarter], x[:, at + quarter:at + half_feats]], 0)
        rows_x[half, plane] = folded.astype(jnp.bfloat16)
    mean = jnp.sum(x, 1, keepdims=True) / feats
    centered = x - mean
    squares = jnp.sum(centered * centered, 1, keepdims=True)
    lane = lax.broadcasted_iota(jnp.int32, (block, LANES), 1)
    stats[me] = jnp.where(lane == 0, mean, squares)

    pl.semaphore_wait(barrier, N - 1)

    def send_rows(half):
        for k in range(1, C):
            pltpu.make_async_remote_copy(
                src_ref=rows_x.at[half, plane], dst_ref=rows_x.at[half, plane],
                send_sem=x_sem.at[0, half], recv_sem=x_sem.at[1, half],
                device_id=device(gx * C + lax.rem(plane + k, C)), device_id_type=MESH,
            ).start()

    send_rows(0)

    def send_stats(rank):
        pltpu.make_async_remote_copy(
            src_ref=stats.at[me], dst_ref=stats.at[me],
            send_sem=stat_sem.at[0], recv_sem=stat_sem.at[1],
            device_id=device(rank), device_id_type=MESH,
        ).start()

    to_all(send_stats)
    send_rows(1)

    for copy in smalls[1:]:
        copy.wait()

    row = lax.broadcasted_iota(jnp.int32, (SEQS * H, LANES), 0)
    place = jnp.where(row < H, pos_ref[0], pos_ref[1]).astype(jnp.float32)
    angle = place * freq_ref[...]
    turns = jnp.floor(angle * (0.5 / math.pi) + 0.5)
    angle = angle - turns * 6.28125
    angle = angle - turns * (4058 / 2097152)
    angle = angle - turns * (2 * math.pi - 6.28125 - 4058 / 2097152)
    cosine, sine = jnp.cos(angle), jnp.sin(angle)

    def turned(t, cos, sin):
        t1, t2 = t[:, :HALF], t[:, HALF:]
        return jnp.concatenate([t1 * cos - t2 * sin, t2 * cos + t1 * sin], 1)

    cos_all = jnp.concatenate([cosine] * C, 0)
    sin_all = jnp.concatenate([sine] * C, 0)

    arrived(stats.at[pl.ds(0, N - 1)], stat_sem.at[1])
    moments = []
    for c in range(C):
        parts = [stats[g * C + c] for g in range(G)]
        means = [p[:, 0:1] for p in parts]
        mean = functools.reduce(jnp.add, means) / G
        squares = functools.reduce(jnp.add, [p[:, 1:2] for p in parts])
        between = functools.reduce(jnp.add, [(m - mean) * (m - mean) for m in means])
        moments.append((mean, lax.rsqrt((squares + feats * between) / (feats * G) + 1e-05)))

    def normalize(half):
        arrived(rows_x.at[half, pl.ds(0, C - 1)], x_sem.at[1, half])
        for pair in range(C // 2):
            lows, highs = [], []
            for c in (2 * pair, 2 * pair + 1):
                mean, scale = moments[c]
                folded = rows_x[half, c].astype(jnp.float32)
                lows.append((folded[:block] - mean) * scale)
                highs.append((folded[block:] - mean) * scale)
            rows = pl.ds(2 * pair * block, 2 * block)
            for at, part in ((half * half_feats, lows), (half * half_feats + quarter, highs)):
                part = jnp.concatenate(part, 0) * gain_ref[pl.ds(at, quarter)][None, :]
                normed[rows, pl.ds(at, quarter)] = part.astype(jnp.bfloat16)

    normalize(0)
    loads[1].wait()
    for h in range(0, H, 2):
        at = slice(h * DH, (h + 2) * DH)
        total[:, at] = jnp.dot(
            normed[:, :half_feats], wq[0, :half_feats, at], preferred_element_type=jnp.float32
        )
    normalize(1)

    loads[0].wait()
    part = jnp.dot(normed[...], wkv[...], preferred_element_type=jnp.float32)
    for rank in range(N):
        kv_send[rank] = part[rank * SEQS:(rank + 1) * SEQS]

    def send_kv(rank):
        pltpu.make_async_remote_copy(
            src_ref=kv_send.at[rank], dst_ref=kv_recv.at[me],
            send_sem=kv_sem.at[0], recv_sem=kv_sem.at[1],
            device_id=device(rank), device_id_type=MESH,
        ).start()

    to_all(send_kv)
    kv_recv[me] = kv_send[me]

    for j in range(chunks):
        if j > 0:
            loads[1 + j].wait()
        if j == 0:
            loads[1 + chunks].start()
            loads[2 + chunks].start()
        loads[3 + chunks + j].start()
        for h in range(0, H, 2):
            at = slice(h * DH, (h + 2) * DH)
            if j == 0:
                part = total[:, at] + jnp.dot(
                    normed[:, half_feats:], wq[j, half_feats:, at],
                    preferred_element_type=jnp.float32,
                )
            else:
                part = jnp.dot(normed[...], wq[j, :, at], preferred_element_type=jnp.float32)
            for i in range(2):
                for side in range(2):
                    at = i * DH + side * HALF
                    spread[side, pl.ds(h + i, count, stride=H), :] = part[:, at:at + HALF]
        tiles = [spread[side].reshape(N, SEQS * H, HALF) for side in range(2)]
        q_send[j] = jnp.concatenate(tiles, 1)

        def send_query(rank):
            pltpu.make_async_remote_copy(
                src_ref=q_send.at[j, rank], dst_ref=q_recv.at[j, me],
                send_sem=q_sem.at[0, j], recv_sem=q_sem.at[1, j],
                device_id=device(rank), device_id_type=MESH,
            ).start()

        to_all(send_query)
        q_recv[j, me] = q_send[j, me]

    arrived(kv_recv.at[pl.ds(0, N - 1)], kv_sem.at[1])
    pieces = []
    for c in range(C):
        pieces.append(functools.reduce(jnp.add, [kv_recv[g * C + c] for g in range(G)]))
    keyval = jnp.concatenate(pieces, 1)
    keyval = jnp.concatenate(
        [jnp.broadcast_to(keyval[i:i + 1], (H, 2 * DH)) for i in range(SEQS)], 0
    )
    keyval = keyval.astype(jnp.bfloat16).astype(jnp.float32)
    rot_key = turned(keyval[:, :DH], cosine, sine).astype(jnp.bfloat16).astype(jnp.float32)
    key_all = jnp.concatenate([rot_key] * C, 0)
    value_all = jnp.concatenate([keyval[:, DH:]] * C, 0)

    loads[1 + chunks].wait()
    loads[2 + chunks].wait()
    rows_all = C * SEQS * H
    row = lax.broadcasted_iota(jnp.int32, (rows_all, SEQS * slots), 0)
    slot = lax.broadcasted_iota(jnp.int32, (rows_all, SEQS * slots), 1)
    second = lax.rem(row, SEQS * H) >= H
    base = jnp.where(second, slots, 0)
    live = (slot >= base) & (slot < base + jnp.where(second, len_ref[1], len_ref[0]))
    scale = DH ** (-0.5)

    for j in range(chunks):
        arrived(q_recv.at[j, pl.ds(0, N - 1)], q_sem.at[1, j])
        blocks = []
        for c in range(C):
            tile = functools.reduce(jnp.add, [q_recv[j, g * C + c] for g in range(G)])
            blocks.append(jnp.concatenate([tile[:SEQS * H], tile[SEQS * H:]], 1))
        query = jnp.concatenate(blocks, 0).astype(jnp.bfloat16).astype(jnp.float32)
        rot_query = turned(query, cos_all, sin_all).astype(jnp.bfloat16)
        scores = lax.dot_general(
            rot_query, kc[...], (((1,), (1,)), ((), ())), preferred_element_type=jnp.float32
        ) * scale
        selfish = jnp.sum(rot_query.astype(jnp.float32) * key_all, 1, keepdims=True) * scale
        masked = jnp.where(live, scores, -1e30)
        peak = jnp.maximum(jnp.max(masked, 1, keepdims=True), selfish)
        expo = jnp.where(live, jnp.exp(masked - peak), 0.0)
        expo_self = jnp.exp(selfish - peak)
        denominator = jnp.sum(expo, 1, keepdims=True) + expo_self
        probs = (expo / denominator).astype(jnp.bfloat16)
        probs_self = (expo_self / denominator).astype(jnp.bfloat16).astype(jnp.float32)
        mixed = jnp.dot(probs, vc[...], preferred_element_type=jnp.float32)
        mixed = mixed + probs_self * value_all
        for c in range(C):
            tile = mixed[c * SEQS * H:(c + 1) * SEQS * H]
            h_send[j, c] = jnp.concatenate([tile[:, :HALF], tile[:, HALF:]], 0).astype(jnp.bfloat16)

        def send_heads(rank):
            pltpu.make_async_remote_copy(
                src_ref=h_send.at[j, rank % C], dst_ref=h_recv.at[j, me],
                send_sem=h_sem.at[0, j], recv_sem=h_sem.at[1, j],
                device_id=device(rank), device_id_type=MESH,
            ).start()

        to_all(send_heads)
        h_recv[j, me] = h_send[j, plane]

    def gather_heads(j):
        arrived(h_recv.at[j, pl.ds(0, N - 1)], h_sem.at[1, j])
        for rank in range(N):
            tile = h_recv[j, rank].astype(jnp.float32)
            for side in range(2):
                spread[side, rank * SEQS * H:(rank + 1) * SEQS * H] = tile[
                    side * SEQS * H:(side + 1) * SEQS * H
                ]
        for h in range(H):
            for side in range(2):
                at = h * DH + side * HALF
                h_rows[j, :, at:at + HALF] = spread[
                    side, pl.ds(h, count, stride=H), :
                ].astype(jnp.bfloat16)

    for j in range(chunks):
        gather_heads(j)
        loads[3 + chunks + j].wait()

        def columns(n, carry):
            at = pl.ds(pl.multiple_of(n * OUT_COLS, OUT_COLS), OUT_COLS)
            part = jnp.dot(h_rows[j], wo[j, :, at], preferred_element_type=jnp.float32)
            if j > 0:
                part = part + total[:, at]
            if j < chunks - 1:
                total[:, at] = part
                return carry
            for c in range(C):
                tile = part[c * block:(c + 1) * block]
                o_send[n, c] = jnp.concatenate(
                    [tile[:, :OUT_COLS // 2], tile[:, OUT_COLS // 2:]], 0
                ).astype(jnp.bfloat16)
            for k in range(1, C):
                other = lax.rem(plane + k, C)
                pltpu.make_async_remote_copy(
                    src_ref=o_send.at[n, other], dst_ref=o_recv.at[n, k - 1],
                    send_sem=o_sem.at[0, n], recv_sem=o_sem.at[1, n],
                    device_id=device(gx * C + other), device_id_type=MESH,
                ).start()
            return carry

        lax.fori_loop(0, out_chunks, columns, 0)

    def finish(n, carry):
        arrived(o_recv.at[n], o_sem.at[1, n])
        summed = o_send[n, plane].astype(jnp.float32)
        for k in range(C - 1):
            summed = summed + o_recv[n, k].astype(jnp.float32)
        low = pl.multiple_of(n * OUT_COLS, OUT_COLS // 2)
        high = pl.multiple_of(n * OUT_COLS + OUT_COLS // 2, OUT_COLS // 2)
        out_ref[:, pl.ds(low, OUT_COLS // 2)] = summed[:block]
        out_ref[:, pl.ds(high, OUT_COLS // 2)] = summed[block:]
        return carry

    lax.fori_loop(0, out_chunks, finish, 0)

    for half in range(2):
        arrived(rows_x.at[half, pl.ds(0, C - 1)], x_sem.at[0, half])
    arrived(stats.at[pl.ds(0, N - 1)], stat_sem.at[0])
    arrived(kv_recv.at[pl.ds(0, N - 1)], kv_sem.at[0])
    for j in range(chunks):
        arrived(q_recv.at[j, pl.ds(0, N - 1)], q_sem.at[0, j])
        arrived(h_recv.at[j, pl.ds(0, N - 1)], h_sem.at[0, j])

    def left(n, carry):
        arrived(o_recv.at[n], o_sem.at[0, n])
        return carry

    lax.fori_loop(0, out_chunks, left, 0)


def fused(
    sizes, hidden_in, ln_gain, w_query, w_keyval, w_output, key_cache, value_cache, lengths, positions
):
    G, Y, Z = sizes
    C = Y * Z
    N = G * C
    block, feats = hidden_in.shape
    count = block * C
    H = CHUNK_HEADS
    chunks = w_query.shape[1] // (H * DH)
    out_cols = w_output.shape[1]
    out_chunks = out_cols // OUT_COLS
    keys = key_cache.reshape(-1, DH)
    values = value_cache.reshape(-1, DH)
    freqs = np.exp(-np.log(10000.0) * np.arange(HALF) / HALF).astype(np.float32)[None, :]
    bf16, f32 = jnp.bfloat16, jnp.float32
    vmem = pl.BlockSpec(memory_space=pltpu.VMEM)
    anywhere = pl.BlockSpec(memory_space=pl.ANY)
    tile = SEQS * H
    return pl.pallas_call(
        functools.partial(layer_kernel, sizes),
        out_shape=pltpu.VMEM((block, out_cols), f32),
        in_specs=[anywhere] * 10,
        out_specs=vmem,
        scratch_shapes=[
            pltpu.VMEM(hidden_in.shape, bf16),
            pltpu.VMEM(ln_gain.shape, f32),
            pltpu.VMEM(freqs.shape, f32),
            pltpu.SMEM(lengths.shape, jnp.int32),
            pltpu.SMEM(positions.shape, jnp.int32),
            pltpu.VMEM((chunks, feats, H * DH), bf16),
            pltpu.VMEM(w_keyval.shape, bf16),
            pltpu.VMEM((chunks, H * DH, out_cols), bf16),
            pltpu.VMEM(keys.shape, bf16),
            pltpu.VMEM(values.shape, bf16),
            pltpu.VMEM((2, C, 2 * block, feats // 4), bf16),
            pltpu.VMEM((N, block, LANES), f32),
            pltpu.VMEM((count, feats), bf16),
            pltpu.VMEM((chunks, N, 2 * tile, HALF), f32),
            pltpu.VMEM((chunks, N, 2 * tile, HALF), f32),
            pltpu.VMEM((N, SEQS, w_keyval.shape[1]), f32),
            pltpu.VMEM((N, SEQS, w_keyval.shape[1]), f32),
            pltpu.VMEM((chunks, C, 2 * tile, HALF), bf16),
            pltpu.VMEM((chunks, N, 2 * tile, HALF), bf16),
            pltpu.VMEM((2, N * tile, HALF), f32),
            pltpu.VMEM((chunks, count, H * DH), bf16),
            pltpu.VMEM((count, out_cols), f32),
            pltpu.VMEM((out_chunks, C, 2 * block, OUT_COLS // 2), bf16),
            pltpu.VMEM((out_chunks, C - 1, 2 * block, OUT_COLS // 2), bf16),
            pltpu.SemaphoreType.DMA((5,)),
            pltpu.SemaphoreType.DMA((3 + 2 * chunks,)),
            pltpu.SemaphoreType.DMA((2, 2)),
            pltpu.SemaphoreType.DMA((2,)),
            pltpu.SemaphoreType.DMA((2,)),
            pltpu.SemaphoreType.DMA((2, chunks)),
            pltpu.SemaphoreType.DMA((2, chunks)),
            pltpu.SemaphoreType.DMA((2, out_chunks)),
        ],
        compiler_params=pltpu.CompilerParams(
            collective_id=0, has_side_effects=True, vmem_limit_bytes=62 * 1024 * 1024
        ),
    )(
        hidden_in, ln_gain, jnp.asarray(freqs), w_query, w_keyval, w_output,
        keys, values, lengths, positions,
    )


def solution(mesh):
    sizes = (mesh.shape["gx"], mesh.shape["gy"], mesh.shape["gz"])

    def layer(*args):
        hidden_in, _, w_query, w_keyval, w_output, key_cache = args[:6]
        fits = (
            key_cache.shape[0] == SEQS
            and hidden_in.shape[0] == 8
            and sizes[1] * sizes[2] % 2 == 0
            and w_keyval.shape[1] * sizes[1] * sizes[2] == 2 * DH
            and hidden_in.shape[1] % (4 * LANES) == 0
            and w_query.shape[1] % (CHUNK_HEADS * DH) == 0
            and w_keyval.shape[1] == LANES
            and w_output.shape[1] % OUT_COLS == 0
        )
        if fits:
            return fused(sizes, *args)
        return per_device(*args)

    in_specs = (
        P(("grp", "gy", "gz"), "gx"),
        P("gx"),
        P("gx", ("gy", "gz")),
        P("gx", ("gy", "gz")),
        P(("gy", "gz"), "gx"),
        P(("grp", "gx", "gy", "gz"), None, None),
        P(("grp", "gx", "gy", "gz"), None, None),
        P(("grp", "gx", "gy", "gz")),
        P(("grp", "gx", "gy", "gz")),
    )
    out_specs = P(("grp", "gy", "gz"), "gx")
    return jax.shard_map(layer, mesh=mesh, in_specs=in_specs, out_specs=out_specs, check_vma=False)
```

```python
import functools
import math

import jax
import jax.numpy as jnp
import numpy as np
from jax import lax
from jax.experimental import pallas as pl
from jax.experimental.pallas import tpu as pltpu
from jax.sharding import PartitionSpec as P

D = 18432
DH = 256
HALF = DH // 2
LANES = 128
MESH = pl.DeviceIdType.MESH
CHUNK_HEADS = 4
OUT_COLS = 1536
SEQS = 2


def rotary(values, places):
    half = values.shape[-1] // 2
    freqs = jnp.exp(-jnp.log(10000.0) * jnp.arange(half, dtype=jnp.float32) / half)
    angles = places.astype(jnp.float32)[:, None] * freqs[None, :]
    while angles.ndim < values.ndim:
        angles = angles[:, None, :]
    cosine = jnp.cos(angles)
    sine = jnp.sin(angles)
    first = values[..., :half]
    second = values[..., half:]
    return jnp.concatenate([first * cosine - second * sine, second * cosine + first * sine], -1)


def attend(query2d, keyval2d, key_cache, value_cache, lengths, positions):
    count = query2d.shape[0]
    heads_here = query2d.shape[1] // DH
    query = query2d.reshape(count, heads_here, DH).astype(jnp.float32)
    rot_query = rotary(query, positions).astype(jnp.bfloat16)
    rot_key = rotary(keyval2d[:, :DH].astype(jnp.float32), positions).astype(jnp.bfloat16)
    new_value = keyval2d[:, DH:]
    scale = DH ** (-0.5)
    scores = (
        jnp.einsum("bhd,bld->bhl", rot_query, key_cache, preferred_element_type=jnp.float32) * scale
    )
    selfish = (
        jnp.einsum("bhd,bd->bh", rot_query, rot_key, preferred_element_type=jnp.float32) * scale
    )
    live = jnp.arange(key_cache.shape[1], dtype=jnp.int32)[None, :] < lengths[:, None]
    live = live[:, None, :]
    masked = jnp.where(live, scores, -1e30)
    peak = jnp.maximum(jnp.max(masked, -1), selfish)
    expo = jnp.where(live, jnp.exp(masked - peak[..., None]), 0.0)
    expo_self = jnp.exp(selfish - peak)
    total = jnp.sum(expo, -1) + expo_self
    probs = (expo / total[..., None]).astype(jnp.bfloat16)
    probs_self = (expo_self / total).astype(jnp.bfloat16)
    mixed = jnp.einsum("bhl,bld->bhd", probs, value_cache, preferred_element_type=jnp.float32)
    mixed = (
        mixed
        + probs_self.astype(jnp.float32)[..., None] * new_value.astype(jnp.float32)[:, None, :]
    )
    return mixed.reshape(count, heads_here * DH).astype(jnp.bfloat16)


def per_device(
    hidden_in, ln_gain, w_query, w_keyval, w_output, key_cache, value_cache, lengths, positions
):
    xf = hidden_in.astype(jnp.float32)
    totals, squares = lax.psum((jnp.sum(xf, 1), jnp.sum(xf * xf, 1)), "gx")
    mean = totals / D
    var = squares / D - mean * mean
    centered = xf - mean[:, None]
    normed = (centered * lax.rsqrt(var + 1e-05)[:, None] * ln_gain[None, :]).astype(jnp.bfloat16)
    all_rows = lax.all_gather(normed, ("gy", "gz"), axis=0, tiled=True)
    query_cols = w_query.shape[1]
    first = jnp.dot(all_rows, w_query, preferred_element_type=jnp.float32)
    second = jnp.dot(all_rows, w_keyval, preferred_element_type=jnp.float32)
    projected = lax.psum_scatter(
        jnp.concatenate([first, second], 1), "gx", scatter_dimension=0, tiled=True
    ).astype(jnp.bfloat16)
    query_part = projected[:, :query_cols]
    keyval_part = projected[:, query_cols:]
    query_seq, keyval_seq = (
        lax.all_to_all(query_part, ("gy", "gz"), split_axis=0, concat_axis=1, tiled=True),
        lax.all_to_all(keyval_part, ("gy", "gz"), split_axis=0, concat_axis=1, tiled=True),
    )
    attended = attend(query_seq, keyval_seq, key_cache, value_cache, lengths, positions)
    head_block = lax.all_to_all(attended, ("gy", "gz"), split_axis=1, concat_axis=0, tiled=True)
    partials = jnp.dot(
        lax.all_gather(head_block, "gx", axis=0, tiled=True),
        w_output,
        preferred_element_type=jnp.float32,
    )
    return lax.psum_scatter(
        partials.astype(jnp.bfloat16), ("gy", "gz"), scatter_dimension=0, tiled=True
    ).astype(jnp.float32)


def layer_kernel(
    sizes,
    x_hbm, gain_hbm, freq_hbm, wq_hbm, wkv_hbm, wo_hbm, kc_hbm, vc_hbm, len_hbm, pos_hbm,
    out_ref,
    x_ref, gain_ref, freq_ref, len_ref, pos_ref,
    wq, wkv, wo, kc, vc,
    rows_x, stats, normed, q_send, q_recv, kv_send, kv_recv,
    h_send, h_recv, spread, h_rows, total, o_send, o_recv,
    small_sem, load_sem, x_sem, stat_sem, kv_sem, q_sem, h_sem, o_sem,
):
    G, Y, Z = sizes
    C = Y * Z
    N = G * C
    H = CHUNK_HEADS
    chunks = wq.shape[0]
    count = 2 * C * G
    feats = x_ref.shape[1]
    half_feats = feats // 2
    quarter = feats // 4
    out_chunks = o_send.shape[0]
    slots = kc.shape[0] // SEQS
    block = x_ref.shape[0]
    gx, gy, gz = (lax.axis_index(axis) for axis in ("gx", "gy", "gz"))
    plane = gy * Z + gz
    me = gx * C + plane

    def device(rank):
        return {"gx": rank // C, "gy": rank % C // Z, "gz": rank % Z}

    def load(j, source, target):
        return pltpu.make_async_copy(source, target, load_sem.at[j])

    def arrived(ref, sem):
        pltpu.make_async_copy(ref, ref, sem).wait()

    def to_all(body):
        def step(k, carry):
            body(lax.rem(me + k, N))
            return carry

        lax.fori_loop(1, N, step, 0)

    barrier = pltpu.get_barrier_semaphore()

    def greet(rank):
        pl.semaphore_signal(barrier, inc=1, device_id=device(rank), device_id_type=MESH)

    to_all(greet)

    smalls = [
        pltpu.make_async_copy(source, target, small_sem.at[i])
        for i, (source, target) in enumerate(
            [(x_hbm, x_ref), (gain_hbm, gain_ref), (freq_hbm, freq_ref),
             (len_hbm, len_ref), (pos_hbm, pos_ref)]
        )
    ]
    for copy in smalls:
        copy.start()
    loads = [load(0, wkv_hbm, wkv)]
    cols = H * DH
    for j in range(chunks):
        loads.append(load(1 + j, wq_hbm.at[:, pl.ds(j * cols, cols)], wq.at[j]))
    loads.append(load(1 + chunks, kc_hbm, kc))
    loads.append(load(2 + chunks, vc_hbm, vc))
    for j in range(chunks):
        loads.append(load(3 + chunks + j, wo_hbm.at[pl.ds(j * cols, cols), :], wo.at[j]))
    for j in range(1 + chunks):
        loads[j].start()

    smalls[0].wait()
    x = x_ref[...].astype(jnp.float32)
    for half in range(2):
        at = half * half_feats
        folded = jnp.concatenate([x[:, at:at + quarter], x[:, at + quarter:at + half_feats]], 0)
        rows_x[half, plane] = folded.astype(jnp.bfloat16)
    mean = jnp.sum(x, 1, keepdims=True) / feats
    centered = x - mean
    squares = jnp.sum(centered * centered, 1, keepdims=True)
    lane = lax.broadcasted_iota(jnp.int32, (block, LANES), 1)
    stats[me] = jnp.where(lane == 0, mean, squares)

    pl.semaphore_wait(barrier, N - 1)

    def send_rows(half):
        for k in range(1, C):
            pltpu.make_async_remote_copy(
                src_ref=rows_x.at[half, plane], dst_ref=rows_x.at[half, plane],
                send_sem=x_sem.at[0, half], recv_sem=x_sem.at[1, half],
                device_id=device(gx * C + lax.rem(plane + k, C)), device_id_type=MESH,
            ).start()

    send_rows(0)

    def send_stats(rank):
        pltpu.make_async_remote_copy(
            src_ref=stats.at[me], dst_ref=stats.at[me],
            send_sem=stat_sem.at[0], recv_sem=stat_sem.at[1],
            device_id=device(rank), device_id_type=MESH,
        ).start()

    to_all(send_stats)
    send_rows(1)

    for copy in smalls[1:]:
        copy.wait()

    row = lax.broadcasted_iota(jnp.int32, (SEQS * H, LANES), 0)
    place = jnp.where(row < H, pos_ref[0], pos_ref[1]).astype(jnp.float32)
    angle = place * freq_ref[...]
    turns = jnp.floor(angle * (0.5 / math.pi) + 0.5)
    angle = angle - turns * 6.28125
    angle = angle - turns * (4058 / 2097152)
    angle = angle - turns * (2 * math.pi - 6.28125 - 4058 / 2097152)
    cosine, sine = jnp.cos(angle), jnp.sin(angle)

    def turned(t, cos, sin):
        t1, t2 = t[:, :HALF], t[:, HALF:]
        return jnp.concatenate([t1 * cos - t2 * sin, t2 * cos + t1 * sin], 1)

    cos_all = jnp.concatenate([cosine] * C, 0)
    sin_all = jnp.concatenate([sine] * C, 0)

    arrived(stats.at[pl.ds(0, N - 1)], stat_sem.at[1])
    moments = []
    for c in range(C):
        parts = [stats[g * C + c] for g in range(G)]
        means = [p[:, 0:1] for p in parts]
        mean = functools.reduce(jnp.add, means) / G
        squares = functools.reduce(jnp.add, [p[:, 1:2] for p in parts])
        between = functools.reduce(jnp.add, [(m - mean) * (m - mean) for m in means])
        moments.append((mean, lax.rsqrt((squares + feats * between) / (feats * G) + 1e-05)))

    def normalize(half):
        arrived(rows_x.at[half, pl.ds(0, C - 1)], x_sem.at[1, half])
        for pair in range(C // 2):
            lows, highs = [], []
            for c in (2 * pair, 2 * pair + 1):
                mean, scale = moments[c]
                folded = rows_x[half, c].astype(jnp.float32)
                lows.append((folded[:block] - mean) * scale)
                highs.append((folded[block:] - mean) * scale)
            rows = pl.ds(2 * pair * block, 2 * block)
            for at, part in ((half * half_feats, lows), (half * half_feats + quarter, highs)):
                part = jnp.concatenate(part, 0) * gain_ref[pl.ds(at, quarter)][None, :]
                normed[rows, pl.ds(at, quarter)] = part.astype(jnp.bfloat16)

    normalize(0)
    loads[1].wait()
    for h in range(0, H, 2):
        at = slice(h * DH, (h + 2) * DH)
        total[:, at] = jnp.dot(
            normed[:, :half_feats], wq[0, :half_feats, at], preferred_element_type=jnp.float32
        )
    normalize(1)

    for j in range(chunks):
        if j > 0:
            loads[1 + j].wait()
        if j == 0:
            loads[1 + chunks].start()
            loads[2 + chunks].start()
        loads[3 + chunks + j].start()
        for h in range(0, H, 2):
            at = slice(h * DH, (h + 2) * DH)
            if j == 0:
                part = total[:, at] + jnp.dot(
                    normed[:, half_feats:], wq[j, half_feats:, at],
                    preferred_element_type=jnp.float32,
                )
            else:
                part = jnp.dot(normed[...], wq[j, :, at], preferred_element_type=jnp.float32)
            for i in range(2):
                for side in range(2):
                    at = i * DH + side * HALF
                    spread[side, pl.ds(h + i, count, stride=H), :] = part[:, at:at + HALF]
        tiles = [spread[side].reshape(N, SEQS * H, HALF) for side in range(2)]
        q_send[j] = jnp.concatenate(tiles, 1)

        def send_query(rank):
            pltpu.make_async_remote_copy(
                src_ref=q_send.at[j, rank], dst_ref=q_recv.at[j, me],
                send_sem=q_sem.at[0, j], recv_sem=q_sem.at[1, j],
                device_id=device(rank), device_id_type=MESH,
            ).start()

        to_all(send_query)
        q_recv[j, me] = q_send[j, me]
        if j == 0:
            loads[0].wait()
            part = jnp.dot(normed[...], wkv[...], preferred_element_type=jnp.float32)
            for rank in range(N):
                kv_send[rank] = part[rank * SEQS:(rank + 1) * SEQS]

            def send_kv(rank):
                pltpu.make_async_remote_copy(
                    src_ref=kv_send.at[rank], dst_ref=kv_recv.at[me],
                    send_sem=kv_sem.at[0], recv_sem=kv_sem.at[1],
                    device_id=device(rank), device_id_type=MESH,
                ).start()

            to_all(send_kv)
            kv_recv[me] = kv_send[me]

    arrived(kv_recv.at[pl.ds(0, N - 1)], kv_sem.at[1])
    pieces = []
    for c in range(C):
        pieces.append(functools.reduce(jnp.add, [kv_recv[g * C + c] for g in range(G)]))
    keyval = jnp.concatenate(pieces, 1)
    keyval = jnp.concatenate(
        [jnp.broadcast_to(keyval[i:i + 1], (H, 2 * DH)) for i in range(SEQS)], 0
    )
    keyval = keyval.astype(jnp.bfloat16).astype(jnp.float32)
    rot_key = turned(keyval[:, :DH], cosine, sine).astype(jnp.bfloat16).astype(jnp.float32)
    key_all = jnp.concatenate([rot_key] * C, 0)
    value_all = jnp.concatenate([keyval[:, DH:]] * C, 0)

    loads[1 + chunks].wait()
    loads[2 + chunks].wait()
    rows_all = C * SEQS * H
    row = lax.broadcasted_iota(jnp.int32, (rows_all, SEQS * slots), 0)
    slot = lax.broadcasted_iota(jnp.int32, (rows_all, SEQS * slots), 1)
    second = lax.rem(row, SEQS * H) >= H
    base = jnp.where(second, slots, 0)
    live = (slot >= base) & (slot < base + jnp.where(second, len_ref[1], len_ref[0]))
    scale = DH ** (-0.5)

    for j in range(chunks):
        arrived(q_recv.at[j, pl.ds(0, N - 1)], q_sem.at[1, j])
        blocks = []
        for c in range(C):
            tile = functools.reduce(jnp.add, [q_recv[j, g * C + c] for g in range(G)])
            blocks.append(jnp.concatenate([tile[:SEQS * H], tile[SEQS * H:]], 1))
        query = jnp.concatenate(blocks, 0).astype(jnp.bfloat16).astype(jnp.float32)
        rot_query = turned(query, cos_all, sin_all).astype(jnp.bfloat16)
        scores = lax.dot_general(
            rot_query, kc[...], (((1,), (1,)), ((), ())), preferred_element_type=jnp.float32
        ) * scale
        selfish = jnp.sum(rot_query.astype(jnp.float32) * key_all, 1, keepdims=True) * scale
        masked = jnp.where(live, scores, -1e30)
        peak = jnp.maximum(jnp.max(masked, 1, keepdims=True), selfish)
        expo = jnp.where(live, jnp.exp(masked - peak), 0.0)
        expo_self = jnp.exp(selfish - peak)
        denominator = jnp.sum(expo, 1, keepdims=True) + expo_self
        probs = (expo / denominator).astype(jnp.bfloat16)
        probs_self = (expo_self / denominator).astype(jnp.bfloat16).astype(jnp.float32)
        mixed = jnp.dot(probs, vc[...], preferred_element_type=jnp.float32)
        mixed = mixed + probs_self * value_all
        for c in range(C):
            tile = mixed[c * SEQS * H:(c + 1) * SEQS * H]
            h_send[j, c] = jnp.concatenate([tile[:, :HALF], tile[:, HALF:]], 0).astype(jnp.bfloat16)

        def send_heads(rank):
            pltpu.make_async_remote_copy(
                src_ref=h_send.at[j, rank % C], dst_ref=h_recv.at[j, me],
                send_sem=h_sem.at[0, j], recv_sem=h_sem.at[1, j],
                device_id=device(rank), device_id_type=MESH,
            ).start()

        to_all(send_heads)
        h_recv[j, me] = h_send[j, plane]

    def gather_heads(j):
        arrived(h_recv.at[j, pl.ds(0, N - 1)], h_sem.at[1, j])
        for rank in range(N):
            tile = h_recv[j, rank].astype(jnp.float32)
            for side in range(2):
                spread[side, rank * SEQS * H:(rank + 1) * SEQS * H] = tile[
                    side * SEQS * H:(side + 1) * SEQS * H
                ]
        for h in range(H):
            for side in range(2):
                at = h * DH + side * HALF
                h_rows[j, :, at:at + HALF] = spread[
                    side, pl.ds(h, count, stride=H), :
                ].astype(jnp.bfloat16)

    for j in range(chunks):
        gather_heads(j)
        loads[3 + chunks + j].wait()

        def columns(n, carry):
            at = pl.ds(pl.multiple_of(n * OUT_COLS, OUT_COLS), OUT_COLS)
            part = jnp.dot(h_rows[j], wo[j, :, at], preferred_element_type=jnp.float32)
            if j > 0:
                part = part + total[:, at]
            if j < chunks - 1:
                total[:, at] = part
                return carry
            for c in range(C):
                tile = part[c * block:(c + 1) * block]
                o_send[n, c] = jnp.concatenate(
                    [tile[:, :OUT_COLS // 2], tile[:, OUT_COLS // 2:]], 0
                ).astype(jnp.bfloat16)
            for k in range(1, C):
                other = lax.rem(plane + k, C)
                pltpu.make_async_remote_copy(
                    src_ref=o_send.at[n, other], dst_ref=o_recv.at[n, k - 1],
                    send_sem=o_sem.at[0, n], recv_sem=o_sem.at[1, n],
                    device_id=device(gx * C + other), device_id_type=MESH,
                ).start()
            return carry

        lax.fori_loop(0, out_chunks, columns, 0)

    def finish(n, carry):
        arrived(o_recv.at[n], o_sem.at[1, n])
        summed = o_send[n, plane].astype(jnp.float32)
        for k in range(C - 1):
            summed = summed + o_recv[n, k].astype(jnp.float32)
        low = pl.multiple_of(n * OUT_COLS, OUT_COLS // 2)
        high = pl.multiple_of(n * OUT_COLS + OUT_COLS // 2, OUT_COLS // 2)
        out_ref[:, pl.ds(low, OUT_COLS // 2)] = summed[:block]
        out_ref[:, pl.ds(high, OUT_COLS // 2)] = summed[block:]
        return carry

    lax.fori_loop(0, out_chunks, finish, 0)

    for half in range(2):
        arrived(rows_x.at[half, pl.ds(0, C - 1)], x_sem.at[0, half])
    arrived(stats.at[pl.ds(0, N - 1)], stat_sem.at[0])
    arrived(kv_recv.at[pl.ds(0, N - 1)], kv_sem.at[0])
    for j in range(chunks):
        arrived(q_recv.at[j, pl.ds(0, N - 1)], q_sem.at[0, j])
        arrived(h_recv.at[j, pl.ds(0, N - 1)], h_sem.at[0, j])

    def left(n, carry):
        arrived(o_recv.at[n], o_sem.at[0, n])
        return carry

    lax.fori_loop(0, out_chunks, left, 0)


def fused(
    sizes, hidden_in, ln_gain, w_query, w_keyval, w_output, key_cache, value_cache, lengths, positions
):
    G, Y, Z = sizes
    C = Y * Z
    N = G * C
    block, feats = hidden_in.shape
    count = block * C
    H = CHUNK_HEADS
    chunks = w_query.shape[1] // (H * DH)
    out_cols = w_output.shape[1]
    out_chunks = out_cols // OUT_COLS
    keys = key_cache.reshape(-1, DH)
    values = value_cache.reshape(-1, DH)
    freqs = np.exp(-np.log(10000.0) * np.arange(HALF) / HALF).astype(np.float32)[None, :]
    bf16, f32 = jnp.bfloat16, jnp.float32
    vmem = pl.BlockSpec(memory_space=pltpu.VMEM)
    anywhere = pl.BlockSpec(memory_space=pl.ANY)
    tile = SEQS * H
    return pl.pallas_call(
        functools.partial(layer_kernel, sizes),
        out_shape=pltpu.VMEM((block, out_cols), f32),
        in_specs=[anywhere] * 10,
        out_specs=vmem,
        scratch_shapes=[
            pltpu.VMEM(hidden_in.shape, bf16),
            pltpu.VMEM(ln_gain.shape, f32),
            pltpu.VMEM(freqs.shape, f32),
            pltpu.SMEM(lengths.shape, jnp.int32),
            pltpu.SMEM(positions.shape, jnp.int32),
            pltpu.VMEM((chunks, feats, H * DH), bf16),
            pltpu.VMEM(w_keyval.shape, bf16),
            pltpu.VMEM((chunks, H * DH, out_cols), bf16),
            pltpu.VMEM(keys.shape, bf16),
            pltpu.VMEM(values.shape, bf16),
            pltpu.VMEM((2, C, 2 * block, feats // 4), bf16),
            pltpu.VMEM((N, block, LANES), f32),
            pltpu.VMEM((count, feats), bf16),
            pltpu.VMEM((chunks, N, 2 * tile, HALF), f32),
            pltpu.VMEM((chunks, N, 2 * tile, HALF), f32),
            pltpu.VMEM((N, SEQS, w_keyval.shape[1]), f32),
            pltpu.VMEM((N, SEQS, w_keyval.shape[1]), f32),
            pltpu.VMEM((chunks, C, 2 * tile, HALF), bf16),
            pltpu.VMEM((chunks, N, 2 * tile, HALF), bf16),
            pltpu.VMEM((2, N * tile, HALF), f32),
            pltpu.VMEM((chunks, count, H * DH), bf16),
            pltpu.VMEM((count, out_cols), f32),
            pltpu.VMEM((out_chunks, C, 2 * block, OUT_COLS // 2), bf16),
            pltpu.VMEM((out_chunks, C - 1, 2 * block, OUT_COLS // 2), bf16),
            pltpu.SemaphoreType.DMA((5,)),
            pltpu.SemaphoreType.DMA((3 + 2 * chunks,)),
            pltpu.SemaphoreType.DMA((2, 2)),
            pltpu.SemaphoreType.DMA((2,)),
            pltpu.SemaphoreType.DMA((2,)),
            pltpu.SemaphoreType.DMA((2, chunks)),
            pltpu.SemaphoreType.DMA((2, chunks)),
            pltpu.SemaphoreType.DMA((2, out_chunks)),
        ],
        compiler_params=pltpu.CompilerParams(
            collective_id=0, has_side_effects=True, vmem_limit_bytes=62 * 1024 * 1024
        ),
    )(
        hidden_in, ln_gain, jnp.asarray(freqs), w_query, w_keyval, w_output,
        keys, values, lengths, positions,
    )


def solution(mesh):
    sizes = (mesh.shape["gx"], mesh.shape["gy"], mesh.shape["gz"])

    def layer(*args):
        hidden_in, _, w_query, w_keyval, w_output, key_cache = args[:6]
        fits = (
            key_cache.shape[0] == SEQS
            and hidden_in.shape[0] == 8
            and sizes[1] * sizes[2] % 2 == 0
            and w_keyval.shape[1] * sizes[1] * sizes[2] == 2 * DH
            and hidden_in.shape[1] % (4 * LANES) == 0
            and w_query.shape[1] % (CHUNK_HEADS * DH) == 0
            and w_keyval.shape[1] == LANES
            and w_output.shape[1] % OUT_COLS == 0
        )
        if fits:
            return fused(sizes, *args)
        return per_device(*args)

    in_specs = (
        P(("grp", "gy", "gz"), "gx"),
        P("gx"),
        P("gx", ("gy", "gz")),
        P("gx", ("gy", "gz")),
        P(("gy", "gz"), "gx"),
        P(("grp", "gx", "gy", "gz"), None, None),
        P(("grp", "gx", "gy", "gz"), None, None),
        P(("grp", "gx", "gy", "gz")),
        P(("grp", "gx", "gy", "gz")),
    )
    out_specs = P(("grp", "gy", "gz"), "gx")
    return jax.shard_map(layer, mesh=mesh, in_specs=in_specs, out_specs=out_specs, check_vma=False)
```
